256 devices in a mesh: seq: 64 (over x, z, core), ch: 4 (over y).
Axes of the slice: x: 4, y: 4, z: 8, core: 2. Of those that a mesh axis runs over, the one named last changes fastest.
Arguments:
- queries: bfloat16 [8192, 2048], P('seq', 'ch'), may hold values from -6 to 6
- key_proj: bfloat16 [8192, 2048], P('seq', 'ch'), may hold values from -6 to 6
- value_proj: bfloat16 [8192, 2048], P('seq', 'ch'), may hold values from -6 to 6
- conv_out: bfloat16 [8192, 2048], P('seq', 'ch'), may hold values from -6 to 6
- filters: bfloat16 [8192, 2048], P('seq', 'ch'), may hold values from -0.0625 to 0.0625
- out_grad: bfloat16 [8192, 2048], P('seq', 'ch'), may hold values from -6 to 6
- out_weight: bfloat16 [2048, 2048], P('seq', 'ch'), may hold values from -0.125 to 0.125
Outputs:
- query_grad: bfloat16 [8192, 2048], P('seq', 'ch')
- key_grad: bfloat16 [8192, 2048], P('seq', 'ch')
- value_grad: bfloat16 [8192, 2048], P('seq', 'ch')
- weight_grad: float32 [2048, 2048], P('seq', 'ch')
The draws below stay inside these ranges and needn't reach their ends.
All inputs are finite; a program needn't handle non-finite values.
Results may differ from the reference program's by a relative error of at most 0.008.
Values may be sent and summed in bfloat16 or wider, within the bound.
No kernel may reach another device: no remote copies, remote signals or barrier semaphores. Data moves between devices by JAX's collectives and lax.ppermute only.
A program may use at most 128 MiB of HBM per device.

```python
import jax
import jax.numpy as jnp

D = 2048
TOKENS = 8192


def block_scale(own_key, extent, shards, least, top_value):
    factor_of, own = 1.0, jax.random.fold_in(own_key, 6)
    for dim, blocks in shards:
        draws = jnp.exp(jax.random.uniform(jax.random.fold_in(own, dim), (blocks,), jnp.float32, least / len(shards), top_value / len(shards)))
        factor_of = factor_of * jnp.repeat(draws, extent[dim] // blocks).reshape([-1 if axis == dim else 1 for axis in range(len(extent))])
    return factor_of


def bell_draw(rng, extent, width, limit, pieces=(), dtype=jnp.bfloat16):
    array = jax.random.normal(rng, extent, jnp.float32) * width
    if len(pieces) > 0:
        array = block_scale(rng, extent, pieces, -0.22, 0.18) * array
    return jnp.clip(array, min=-limit, max=limit).astype(dtype)


def setup_inputs(seed: int = 0) -> dict:
    splits = jax.random.split(jax.random.key(seed), 8)
    return {
        "queries": bell_draw(splits[0], (TOKENS, D), 1.0, 6.0, ((0, 64), (1, 4))),
        "key_proj": bell_draw(splits[1], (TOKENS, D), 1.0, 6.0, ((0, 64), (1, 4))),
        "value_proj": bell_draw(splits[2], (TOKENS, D), 1.0, 6.0, ((0, 64), (1, 4))),
        "conv_out": bell_draw(splits[3], (TOKENS, D), 1.0, 6.0, ((0, 64), (1, 4))),
        "filters": bell_draw(splits[4], (TOKENS, D), TOKENS ** -0.5, 0.0625, ((0, 64), (1, 4))),
        "out_grad": bell_draw(splits[5], (TOKENS, D), 1.0, 6.0, ((0, 64), (1, 4))),
        "out_weight": bell_draw(splits[6], (D, D), D ** -0.5, 0.125, ((0, 64), (1, 4))),
    }


def reference(queries, key_proj, value_proj, conv_out, filters, out_grad, out_weight):
    grad_gate = jnp.dot(out_grad, out_weight, preferred_element_type=jnp.float32)
    gated = (queries.astype(jnp.float32) * conv_out.astype(jnp.float32)).astype(jnp.bfloat16)
    weight_grad = jnp.dot(out_grad.T, gated, preferred_element_type=jnp.float32) * (TOKENS ** -0.5)
    query_grad = (grad_gate * conv_out.astype(jnp.float32)).astype(jnp.bfloat16)
    conv_grad = (grad_gate * queries.astype(jnp.float32)).astype(jnp.bfloat16)
    period = 2 * TOKENS
    grad_spec = jnp.fft.rfft(conv_grad.astype(jnp.float32), n=period, axis=0)
    filt_spec = jnp.fft.rfft(filters.astype(jnp.float32), n=period, axis=0)
    inner = jnp.fft.irfft(grad_spec * jnp.conj(filt_spec), n=period, axis=0)[:TOKENS]
    inner = inner.astype(jnp.float32)
    key_grad = (inner * value_proj.astype(jnp.float32)).astype(jnp.bfloat16)
    value_grad = (inner * key_proj.astype(jnp.float32)).astype(jnp.bfloat16)
    return query_grad, key_grad, value_grad, weight_grad
```

```python
import functools

import jax
import jax.numpy as jnp
import numpy as np
from jax import lax
from jax.experimental import pallas as pl
from jax.experimental.pallas import tpu as pltpu
from jax.sharding import PartitionSpec as P

BF16 = jnp.bfloat16
F32 = jnp.float32

CORES = 2


def core_pairs(groups):
    return [(i, i ^ 1) for i in range(groups)]


def same_core_groups(groups):
    return [list(range(core, groups, CORES)) for core in range(CORES)]


def dft_tables(blocks, rows, kept):
    period = 2 * blocks
    length = period * rows
    k1 = np.arange(kept)[:, None]
    used = k1 <= blocks
    angle = 2 * np.pi * ((k1 * np.arange(blocks)[None]) % period) / period
    first = np.concatenate([used * np.cos(angle), used * -np.sin(angle)], 0)
    weight = used * np.where((k1 == 0) | (k1 == blocks), 1.0, 2.0) / length
    last = np.concatenate([(weight * np.cos(angle)).T, -(weight * np.sin(angle)).T], 1)
    turn = 2 * np.pi * (k1 * np.arange(rows)[None]) / length
    twist = np.stack([np.cos(turn), -np.sin(turn)])
    angle = 2 * np.pi * ((np.arange(rows)[:, None] * np.arange(rows)[None]) % rows) / rows
    cos, sin = np.cos(angle), np.sin(angle)
    second = np.block([[cos, -sin], [sin, cos]])
    return first, twist, second, last


def halves(table):
    high = table.astype(BF16)
    low = (table - high.astype(np.float64)).astype(BF16)
    return high, low


def split(value):
    high = value.astype(BF16)
    return high, (value - high.astype(F32)).astype(BF16)


def dot(a, b):
    return jnp.dot(a, b, preferred_element_type=F32)


def dot3(a, b):
    return dot(a[0], b[0]) + (dot(a[0], b[1]) + dot(a[1], b[0]))


def spectrum(x_ref, first_ref, twist_ref, second_ref, plane, blocks, chans, rows, kept):
    plane[...] = x_ref[...].astype(F32)
    data = jnp.concatenate(
        [plane[pl.ds(c, blocks, stride=chans), :] for c in range(chans)], 1
    ).astype(BF16)
    bins = dot(first_ref[0], data) + dot(first_ref[1], data)
    cos, sin = twist_ref[0], twist_ref[1]
    parts = []
    for c in range(chans):
        re = bins[:kept, c * rows : (c + 1) * rows]
        im = bins[kept:, c * rows : (c + 1) * rows]
        parts.append(jnp.concatenate([re * cos - im * sin, re * sin + im * cos], 1))
    return dot3(split(jnp.concatenate(parts, 0)), (second_ref[0], second_ref[1]))


def filter_kernel(sizes, x_ref, first_ref, twist_ref, second_ref, out_ref, plane):
    out_ref[...] = spectrum(x_ref, first_ref, twist_ref, second_ref, plane, *sizes)


def correlate_kernel(
    sizes, x_ref, filt_ref, first_ref, twist_ref, second_ref, back_ref, last_ref, out_ref, plane
):
    blocks, chans, rows, kept = sizes
    grads = spectrum(x_ref, first_ref, twist_ref, second_ref, plane, *sizes)
    g_re, g_im = grads[:, :rows], grads[:, rows:]
    f_re, f_im = filt_ref[:, :rows], filt_ref[:, rows:]
    product = jnp.concatenate([g_re * f_re + g_im * f_im, g_im * f_re - g_re * f_im], 1)
    bins = dot3(split(product), (back_ref[0], back_ref[1]))
    cos, sin = twist_ref[0], twist_ref[1]
    parts = []
    for c in range(chans):
        re = bins[c * kept : (c + 1) * kept, :rows]
        im = bins[c * kept : (c + 1) * kept, rows:]
        parts.append(jnp.concatenate([re * cos + im * sin, im * cos - re * sin], 0))
    inner = dot3((last_ref[0], last_ref[1]), split(jnp.concatenate(parts, 1)))
    for c in range(chans):
        plane[pl.ds(c, blocks, stride=chans), :] = inner[:, c * rows : (c + 1) * rows]
    out_ref[...] = plane[...].astype(BF16)


def whole(count):
    return [pl.BlockSpec(memory_space=pltpu.VMEM)] * count


def shards(queries, key_proj, value_proj, conv_out, filters, out_grad, out_weight):
    rows, chan = queries.shape
    groups = lax.axis_size("seq")
    feats = out_weight.shape[0]
    chips = groups // CORES
    chans = chan // groups
    kept = -(-(groups + 1) // 8) * 8
    sizes = (groups, chans, rows, kept)
    odd = lax.axis_index("seq") % CORES == 1
    to_core = functools.partial(lax.ppermute, axis_name="seq", perm=core_pairs(groups))
    same_core = same_core_groups(groups)

    first, twist, second, last = dft_tables(groups, rows, kept)
    first, last = jnp.stack(halves(first)), jnp.stack(halves(last))
    second, back = jnp.stack(halves(second)), jnp.stack(halves(second.T))
    twist = jnp.asarray(twist, F32)

    def exchange(blocks):
        return lax.all_to_all(blocks.reshape(groups, chans, rows), "seq", 0, 0).reshape(chan, rows)

    copies = jnp.broadcast_to(out_weight[None], (chips, feats, chan))
    weight = lax.all_to_all(copies, "seq", 0, 0, axis_index_groups=same_core).reshape(-1, chan)

    wide = lax.all_gather(out_grad.T, "ch", axis=0).reshape(chips, CORES, feats, rows)
    own = jnp.where(odd, wide[:, 1], wide[:, 0]).reshape(chips * feats, rows)
    other = jnp.where(odd, wide[:, 0], wide[:, 1]).reshape(chips * feats, rows)
    grads = jnp.concatenate([own, to_core(other)], 1)

    filt = pl.pallas_call(
        functools.partial(filter_kernel, sizes),
        out_shape=jax.ShapeDtypeStruct((chans * kept, 2 * rows), F32),
        in_specs=whole(4),
        out_specs=pl.BlockSpec(memory_space=pltpu.VMEM),
        scratch_shapes=[pltpu.VMEM((chan, rows), F32)],
        compiler_params=pltpu.CompilerParams(vmem_limit_bytes=32 << 20),
    )(exchange(filters.T), first, twist, second)

    share = lax.dot_general(grads, weight, (((0,), (0,)), ((), ())), preferred_element_type=F32)
    grad_gate = share[:rows] + to_core(share[rows:])
    query_grad = (grad_gate * conv_out.astype(F32)).astype(BF16)
    conv_grad = (grad_gate * queries.astype(F32)).astype(BF16)

    inner = pl.pallas_call(
        functools.partial(correlate_kernel, sizes),
        out_shape=jax.ShapeDtypeStruct((chan, rows), BF16),
        in_specs=whole(7),
        out_specs=pl.BlockSpec(memory_space=pltpu.VMEM),
        scratch_shapes=[pltpu.VMEM((chan, rows), F32)],
        compiler_params=pltpu.CompilerParams(vmem_limit_bytes=32 << 20),
    )(exchange(conv_grad.T), filt, first, twist, second, back, last)
    inner = exchange(inner).T.astype(F32)
    key_grad = (inner * value_proj.astype(F32)).astype(BF16)
    value_grad = (inner * key_proj.astype(F32)).astype(BF16)

    gated = (queries.astype(F32) * conv_out.astype(F32)).astype(BF16)
    both = jnp.concatenate([gated, to_core(gated)], 0)
    part = dot(grads, both).astype(BF16).reshape(chips, feats, chan)
    parts = lax.all_to_all(part, "seq", 0, 0, axis_index_groups=same_core)
    weight_grad = jnp.sum(parts.astype(F32), 0) * (rows * groups) ** (-0.5)
    return (query_grad, key_grad, value_grad, weight_grad)


def solution(mesh):
    placed = (P("seq", "ch"),) * 7
    return jax.shard_map(
        shards,
        mesh=mesh,
        in_specs=placed,
        out_specs=(P("seq", "ch"),) * 4,
        check_vma=False,
    )
```

```python
import functools

import jax
import jax.numpy as jnp
import numpy as np
from jax import lax
from jax.experimental import pallas as pl
from jax.experimental.pallas import tpu as pltpu
from jax.sharding import PartitionSpec as P

BF16 = jnp.bfloat16
F32 = jnp.float32

CORES = 2
ALONG_X = 4


def core_pairs(groups):
    return [(i, i ^ 1) for i in range(groups)]


def dft_tables(blocks, rows, kept):
    period = 2 * blocks
    length = period * rows
    k1 = np.arange(kept)[:, None]
    used = k1 <= blocks
    angle = 2 * np.pi * ((k1 * np.arange(blocks)[None]) % period) / period
    first = np.concatenate([used * np.cos(angle), used * -np.sin(angle)], 0)
    weight = used * np.where((k1 == 0) | (k1 == blocks), 1.0, 2.0) / length
    last = np.concatenate([(weight * np.cos(angle)).T, -(weight * np.sin(angle)).T], 1)
    turn = 2 * np.pi * (k1 * np.arange(rows)[None]) / length
    twist = np.stack([np.cos(turn), -np.sin(turn)])
    angle = 2 * np.pi * ((np.arange(rows)[:, None] * np.arange(rows)[None]) % rows) / rows
    cos, sin = np.cos(angle), np.sin(angle)
    second = np.block([[cos, -sin], [sin, cos]])
    return first, twist, second, last


def halves(table):
    high = table.astype(BF16)
    low = (table - high.astype(np.float64)).astype(BF16)
    return high, low


def split(value):
    high = value.astype(BF16)
    return high, (value - high.astype(F32)).astype(BF16)


def dot(a, b):
    return jnp.dot(a, b, preferred_element_type=F32)


def dot3(a, b):
    return dot(a[0], b[0]) + (dot(a[0], b[1]) + dot(a[1], b[0]))


def spectrum(x_ref, first_ref, twist_ref, second_ref, plane, blocks, chans, rows, kept):
    plane[...] = x_ref[...].astype(F32)
    data = jnp.concatenate(
        [plane[pl.ds(c, blocks, stride=chans), :] for c in range(chans)], 1
    ).astype(BF16)
    bins = dot(first_ref[0], data) + dot(first_ref[1], data)
    cos, sin = twist_ref[0], twist_ref[1]
    parts = []
    for c in range(chans):
        re = bins[:kept, c * rows : (c + 1) * rows]
        im = bins[kept:, c * rows : (c + 1) * rows]
        parts.append(jnp.concatenate([re * cos - im * sin, re * sin + im * cos], 1))
    return dot3(split(jnp.concatenate(parts, 0)), (second_ref[0], second_ref[1]))


def filter_kernel(sizes, x_ref, first_ref, twist_ref, second_ref, out_ref, plane):
    out_ref[...] = spectrum(x_ref, first_ref, twist_ref, second_ref, plane, *sizes)


def correlate_kernel(
    sizes, x_ref, filt_ref, first_ref, twist_ref, second_ref, back_ref, last_ref, out_ref, plane
):
    blocks, chans, rows, kept = sizes
    grads = spectrum(x_ref, first_ref, twist_ref, second_ref, plane, *sizes)
    g_re, g_im = grads[:, :rows], grads[:, rows:]
    f_re, f_im = filt_ref[:, :rows], filt_ref[:, rows:]
    product = jnp.concatenate([g_re * f_re + g_im * f_im, g_im * f_re - g_re * f_im], 1)
    bins = dot3(split(product), (back_ref[0], back_ref[1]))
    cos, sin = twist_ref[0], twist_ref[1]
    parts = []
    for c in range(chans):
        re = bins[c * kept : (c + 1) * kept, :rows]
        im = bins[c * kept : (c + 1) * kept, rows:]
        parts.append(jnp.concatenate([re * cos + im * sin, im * cos - re * sin], 0))
    inner = dot3((last_ref[0], last_ref[1]), split(jnp.concatenate(parts, 1)))
    for c in range(chans):
        plane[pl.ds(c, blocks, stride=chans), :] = inner[:, c * rows : (c + 1) * rows]
    out_ref[...] = plane[...].astype(BF16)


def gate_kernel(left_ref, arrived_ref, mine_ref, theirs_ref):
    sources, feats = arrived_ref.shape[0], left_ref.shape[1] // arrived_ref.shape[0]
    weight = arrived_ref[:, :feats, :].reshape(sources * feats, arrived_ref.shape[2])
    share = dot(left_ref[...], weight)
    rows = mine_ref.shape[0]
    mine_ref[...] = share[:rows]
    theirs_ref[...] = share[rows:]


def whole(count):
    return [pl.BlockSpec(memory_space=pltpu.VMEM)] * count


def shards(queries, key_proj, value_proj, conv_out, filters, out_grad, out_weight):
    rows, chan = queries.shape
    groups = lax.axis_size("seq")
    feats = out_weight.shape[0]
    chips = groups // CORES
    half = chan // CORES
    chans = chan // groups
    kept = -(-(groups + 1) // 8) * 8
    sizes = (groups, chans, rows, kept)
    odd = lax.axis_index("seq") % CORES == 1
    to_core = functools.partial(lax.ppermute, axis_name="seq", perm=core_pairs(groups))

    first, twist, second, last = dft_tables(groups, rows, kept)
    first, last = jnp.stack(halves(first)), jnp.stack(halves(last))
    second, back = jnp.stack(halves(second)), jnp.stack(halves(second.T))
    twist = jnp.asarray(twist, F32)

    def exchange(blocks):
        return lax.all_to_all(blocks.reshape(groups, chans, rows), "seq", 0, 0).reshape(chan, rows)

    def other_half(value):
        return jnp.where(odd, value[:, :half], value[:, half:])

    def own_half(value):
        return jnp.where(odd, value[:, half:], value[:, :half])

    copies = jnp.broadcast_to(
        out_weight.reshape(feats, CORES, half).transpose(1, 0, 2)[None], (chips, CORES, feats, half)
    ).reshape(groups, feats, half)
    sent = jnp.pad(filters.T.reshape(groups, chans, rows), ((0, 0), (0, 0), (0, half - rows)))
    arrived = lax.all_to_all(jnp.concatenate([copies, sent], 1), "seq", 0, 0)

    wide = lax.all_gather(out_grad.T, "ch", axis=0, tiled=True)
    grads = jnp.concatenate([wide, to_core(wide)], 1)

    filt = pl.pallas_call(
        functools.partial(filter_kernel, sizes),
        out_shape=jax.ShapeDtypeStruct((chans * kept, 2 * rows), F32),
        in_specs=whole(4),
        out_specs=pl.BlockSpec(memory_space=pltpu.VMEM),
        scratch_shapes=[pltpu.VMEM((chan, rows), F32)],
        compiler_params=pltpu.CompilerParams(vmem_limit_bytes=32 << 20),
    )(arrived[:, feats:, :rows].reshape(chan, rows), first, twist, second)

    mine, theirs = pl.pallas_call(
        gate_kernel,
        out_shape=[jax.ShapeDtypeStruct((rows, half), F32)] * 2,
        in_specs=whole(2),
        out_specs=whole(2),
        compiler_params=pltpu.CompilerParams(vmem_limit_bytes=32 << 20),
    )(grads.T, arrived)
    theirs = to_core(theirs)
    grad_gate = jnp.concatenate(
        [jnp.where(odd, theirs, mine), jnp.where(odd, mine, theirs)], 1
    )
    query_grad = (grad_gate * conv_out.astype(F32)).astype(BF16)
    conv_grad = (grad_gate * queries.astype(F32)).astype(BF16)

    inner = pl.pallas_call(
        functools.partial(correlate_kernel, sizes),
        out_shape=jax.ShapeDtypeStruct((chan, rows), BF16),
        in_specs=whole(7),
        out_specs=pl.BlockSpec(memory_space=pltpu.VMEM),
        scratch_shapes=[pltpu.VMEM((chan, rows), F32)],
        compiler_params=pltpu.CompilerParams(vmem_limit_bytes=32 << 20),
    )(exchange(conv_grad.T), filt, first, twist, second, back, last)
    inner = exchange(inner).T.astype(F32)
    key_grad = (inner * value_proj.astype(F32)).astype(BF16)
    value_grad = (inner * key_proj.astype(F32)).astype(BF16)

    gated = (queries.astype(F32) * conv_out.astype(F32)).astype(BF16)
    both = jnp.concatenate([own_half(gated), to_core(other_half(gated))], 0)
    along_z = chips // ALONG_X
    by_z = grads.reshape(ALONG_X, along_z, CORES * feats, CORES * rows).swapaxes(0, 1)
    part = dot(by_z.reshape(groups * feats, CORES * rows), both)
    z_lines = [
        [(x * along_z + z) * CORES + core for z in range(along_z)]
        for x in range(ALONG_X)
        for core in range(CORES)
    ]
    part = lax.psum_scatter(
        part, "seq", scatter_dimension=0, tiled=True, axis_index_groups=z_lines
    ).reshape(ALONG_X, CORES * feats, half)
    x_place = lax.axis_index("seq") // (along_z * CORES)
    total = lax.dynamic_index_in_dim(part, x_place, 0, keepdims=False)
    step = along_z * CORES
    for hop in range(1, ALONG_X):
        block = lax.dynamic_index_in_dim(part, (x_place + hop) % ALONG_X, 0, keepdims=False)
        total += lax.ppermute(
            block, "seq", [(i, (i + hop * step) % groups) for i in range(groups)]
        )
    total = total.reshape(CORES, feats, half)
    own = jnp.where(odd, total[1], total[0])
    beside = to_core(jnp.where(odd, total[0], total[1]))
    weight_grad = jnp.concatenate([jnp.where(odd, beside, own), jnp.where(odd, own, beside)], 1)
    weight_grad = weight_grad * (rows * groups) ** (-0.5)
    return (query_grad, key_grad, value_grad, weight_grad)


def solution(mesh):
    placed = (P("seq", "ch"),) * 7
    return jax.shard_map(
        shards,
        mesh=mesh,
        in_specs=placed,
        out_specs=(P("seq", "ch"),) * 4,
        check_vma=False,
    )
```

```python
import functools

import jax
import jax.numpy as jnp
import numpy as np
from jax import lax
from jax.experimental import pallas as pl
from jax.experimental.pallas import tpu as pltpu
from jax.sharding import PartitionSpec as P

BF16 = jnp.bfloat16
F32 = jnp.float32

CORES = 2
ALONG_X = 4


def dft_tables(blocks, rows, kept):
    period = 2 * blocks
    length = period * rows
    k1 = np.arange(kept)[:, None]
    used = k1 <= blocks
    angle = 2 * np.pi * ((k1 * np.arange(blocks)[None]) % period) / period
    first = np.concatenate([used * np.cos(angle), used * -np.sin(angle)], 0)
    weight = used * np.where((k1 == 0) | (k1 == blocks), 1.0, 2.0) / length
    last = np.concatenate([(weight * np.cos(angle)).T, -(weight * np.sin(angle)).T], 1)
    turn = 2 * np.pi * (k1 * np.arange(rows)[None]) / length
    twist = np.stack([np.cos(turn), -np.sin(turn)])
    angle = 2 * np.pi * ((np.arange(rows)[:, None] * np.arange(rows)[None]) % rows) / rows
    cos, sin = np.cos(angle), np.sin(angle)
    second = np.block([[cos, -sin], [sin, cos]])
    return first, twist, second, last


def halves(table):
    high = table.astype(BF16)
    low = (table - high.astype(np.float64)).astype(BF16)
    return high, low


def split(value):
    high = value.astype(BF16)
    return high, (value - high.astype(F32)).astype(BF16)


def dot(a, b):
    return jnp.dot(a, b, preferred_element_type=F32)


def dot3(a, b):
    return dot(a[0], b[0]) + (dot(a[0], b[1]) + dot(a[1], b[0]))


def spectrum(x_ref, first_ref, twist_ref, second_ref, plane, blocks, chans, rows, kept):
    plane[...] = x_ref[...].astype(F32)
    data = jnp.concatenate(
        [plane[pl.ds(c, blocks, stride=chans), :] for c in range(chans)], 1
    ).astype(BF16)
    bins = dot(first_ref[0], data) + dot(first_ref[1], data)
    cos, sin = twist_ref[0], twist_ref[1]
    parts = []
    for c in range(chans):
        re = bins[:kept, c * rows : (c + 1) * rows]
        im = bins[kept:, c * rows : (c + 1) * rows]
        parts.append(jnp.concatenate([re * cos - im * sin, re * sin + im * cos], 1))
    return dot3(split(jnp.concatenate(parts, 0)), (second_ref[0], second_ref[1]))


def filter_kernel(sizes, x_ref, first_ref, twist_ref, second_ref, out_ref, plane):
    out_ref[...] = spectrum(x_ref, first_ref, twist_ref, second_ref, plane, *sizes)


def correlate_kernel(
    sizes, x_ref, filt_ref, first_ref, twist_ref, second_ref, back_ref, last_ref, out_ref, plane
):
    blocks, chans, rows, kept = sizes
    grads = spectrum(x_ref, first_ref, twist_ref, second_ref, plane, *sizes)
    g_re, g_im = grads[:, :rows], grads[:, rows:]
    f_re, f_im = filt_ref[:, :rows], filt_ref[:, rows:]
    product = jnp.concatenate([g_re * f_re + g_im * f_im, g_im * f_re - g_re * f_im], 1)
    bins = dot3(split(product), (back_ref[0], back_ref[1]))
    cos, sin = twist_ref[0], twist_ref[1]
    parts = []
    for c in range(chans):
        re = bins[c * kept : (c + 1) * kept, :rows]
        im = bins[c * kept : (c + 1) * kept, rows:]
        parts.append(jnp.concatenate([re * cos + im * sin, im * cos - re * sin], 0))
    inner = dot3((last_ref[0], last_ref[1]), split(jnp.concatenate(parts, 1)))
    for c in range(chans):
        plane[pl.ds(c, blocks, stride=chans), :] = inner[:, c * rows : (c + 1) * rows]
    out_ref[...] = plane[...].astype(BF16)


def pack_kernel(filters_ref, weight_ref, out_ref):
    groups, _, rows = out_ref.shape
    chan = filters_ref.shape[1]
    chans = chan // groups
    feats = weight_ref.shape[0]
    part = chan // (ALONG_X * CORES)
    turned = filters_ref[...].astype(F32).T.astype(BF16)
    out_ref[:, feats // 2 :, :] = turned.reshape(groups, chans, rows)
    weight = weight_ref[...].astype(F32)
    for x in range(ALONG_X):
        for core in range(CORES):
            start = (core * ALONG_X + x) * part
            piece = weight[:, start : start + part]
            folded = jnp.concatenate([piece[: feats // 2], piece[feats // 2 :]], 1).astype(BF16)
            for dest in range(x * groups // ALONG_X + core, (x + 1) * groups // ALONG_X, CORES):
                out_ref[dest, : feats // 2, :] = folded


def gate_kernel(x_ref, left_ref, w0_ref, w1_ref, w2_ref, w3_ref, mine_ref, theirs_ref):
    folded = jnp.concatenate([w0_ref[...], w1_ref[...], w2_ref[...], w3_ref[...]], 1)
    depth = folded.shape[0]
    low = dot(left_ref[:, :depth], folded)
    high = dot(left_ref[:, depth:], folded)
    rows, half = mine_ref.shape
    part = half // ALONG_X
    pieces = [
        low[:, 2 * hop * part : (2 * hop + 1) * part]
        + high[:, (2 * hop + 1) * part : (2 * hop + 2) * part]
        for hop in range(ALONG_X)
    ]
    placed = []
    for x in range(ALONG_X):
        away = (x_ref[0] - x + ALONG_X) % ALONG_X
        value = pieces[0]
        for hop in range(1, ALONG_X):
            value = jnp.where(away == hop, pieces[hop], value)
        placed.append(value)
    share = jnp.concatenate(placed, 1)
    mine_ref[...] = share[:rows]
    theirs_ref[...] = share[rows:]


def grads_kernel(odd_ref, mine_ref, theirs_ref, queries_ref, conv_ref, query_grad_ref, turned_ref):
    odd = odd_ref[0] == 1
    mine, theirs = mine_ref[...], theirs_ref[...]
    gate = jnp.concatenate([jnp.where(odd, theirs, mine), jnp.where(odd, mine, theirs)], 1)
    query_grad_ref[...] = (gate * conv_ref[...].astype(F32)).astype(BF16)
    conv_grad = (gate * queries_ref[...].astype(F32)).astype(BF16)
    turned_ref[...] = conv_grad.astype(F32).T.astype(BF16)


def outputs_kernel(inner_ref, key_ref, value_ref, key_grad_ref, value_grad_ref):
    inner = inner_ref[...].astype(F32).T
    key_grad_ref[...] = (inner * value_ref[...].astype(F32)).astype(BF16)
    value_grad_ref[...] = (inner * key_ref[...].astype(F32)).astype(BF16)


def weight_kernel(x_ref, grads_ref, both_ref, own_ref, *away_refs):
    feats = own_ref.shape[0]
    for hop, out_ref in enumerate((own_ref, *away_refs)):
        start = pl.multiple_of(lax.rem(x_ref[0] + hop, ALONG_X) * feats, feats)
        out_ref[...] = dot(grads_ref[pl.ds(start, feats), :], both_ref[...]).astype(out_ref.dtype)


def in_vmem(count):
    return [pl.BlockSpec(memory_space=pltpu.VMEM)] * count


def call(kernel, out, scalars, *operands, scratch=()):
    return pl.pallas_call(
        kernel,
        out_shape=[jax.ShapeDtypeStruct(shape, dtype) for shape, dtype in out],
        in_specs=[pl.BlockSpec(memory_space=pltpu.SMEM)] * len(scalars) + in_vmem(len(operands)),
        out_specs=in_vmem(len(out)),
        scratch_shapes=[pltpu.VMEM(shape, F32) for shape in scratch],
        compiler_params=pltpu.CompilerParams(vmem_limit_bytes=32 << 20),
    )(*scalars, *operands)


def shards(queries, key_proj, value_proj, conv_out, filters, out_grad, out_weight):
    rows, chan = queries.shape
    groups = lax.axis_size("seq")
    feats = out_weight.shape[0]
    chips = groups // CORES
    along_z = chips // ALONG_X
    half = chan // CORES
    chans = chan // groups
    kept = -(-(groups + 1) // 8) * 8
    sizes = (groups, chans, rows, kept)

    place = lax.axis_index("seq")
    odd = place % CORES == 1
    x_place = place // (along_z * CORES)
    z_place = place // CORES % along_z
    x_scalar = x_place.reshape(1)
    odd_scalar = odd.astype(jnp.int32).reshape(1)

    def send(value, dx, dz, core):
        pairs = []
        for i in range(groups):
            x, z, c = i // (along_z * CORES), i // CORES % along_z, i % CORES
            x, z, c = (x + dx) % ALONG_X, (z + dz) % along_z, c ^ core
            pairs.append((i, (x * along_z + z) * CORES + c))
        return lax.ppermute(value, "seq", pairs)

    def to_core(value):
        return send(value, 0, 0, 1)

    first, twist, second, last = dft_tables(groups, rows, kept)
    first, last = jnp.stack(halves(first)), jnp.stack(halves(last))
    second, back = jnp.stack(halves(second)), jnp.stack(halves(second.T))
    twist = jnp.asarray(twist, F32)

    def exchange(blocks):
        return lax.all_to_all(blocks.reshape(groups, chans, rows), "seq", 0, 0).reshape(chan, rows)

    (packed,) = call(pack_kernel, [((groups, feats // 2 + chans, rows), BF16)], (), filters, out_weight)
    arrived = lax.all_to_all(packed, "seq", 0, 0)
    folded = arrived[:, : feats // 2].reshape(groups * feats // 2, rows)
    weights = [folded] + [send(folded, hop, 0, 0) for hop in range(1, ALONG_X)]
    (filt,) = call(
        functools.partial(filter_kernel, sizes),
        [((chans * kept, 2 * rows), F32)],
        (),
        arrived[:, feats // 2 :].reshape(chan, rows),
        first,
        twist,
        second,
        scratch=[(chan, rows)],
    )

    wide = lax.all_gather(out_grad.T, "ch", axis=0, tiled=True)
    grads = jnp.concatenate([wide, to_core(wide)], 1)
    left = grads.reshape(groups, 2, feats // 2, CORES * rows).transpose(3, 1, 0, 2)

    mine, theirs = call(
        gate_kernel,
        [((rows, half), F32)] * 2,
        (x_scalar,),
        left.reshape(CORES * rows, groups * feats),
        *weights,
    )
    query_grad, turned = call(
        grads_kernel,
        [((rows, chan), BF16), ((chan, rows), BF16)],
        (odd_scalar,),
        mine,
        to_core(theirs),
        queries,
        conv_out,
    )
    (inner,) = call(
        functools.partial(correlate_kernel, sizes),
        [((chan, rows), BF16)],
        (),
        exchange(turned),
        filt,
        first,
        twist,
        second,
        back,
        last,
        scratch=[(chan, rows)],
    )
    key_grad, value_grad = call(
        outputs_kernel, [((rows, chan), BF16)] * 2, (), exchange(inner), key_proj, value_proj
    )

    gated = (queries.astype(F32) * conv_out.astype(F32)).astype(BF16)
    own_half = jnp.where(odd, gated[:, half:], gated[:, :half])
    other_half = jnp.where(odd, gated[:, :half], gated[:, half:])
    both = jnp.concatenate([own_half, to_core(other_half)], 0)
    block = groups * feats // ALONG_X
    total, *away = call(
        weight_kernel,
        [((block, half), F32)] + [((block, half), BF16)] * (ALONG_X - 1),
        (x_scalar,),
        grads,
        both,
    )
    for hop, value in enumerate(away, 1):
        total += send(value, hop, 0, 0).astype(F32)
    quads = along_z // 2
    total = total.reshape(quads, 2 * CORES * feats, half)
    quad = z_place // 2
    part = lax.dynamic_index_in_dim(total, quad, 0, keepdims=False)
    for hop in range(1, quads):
        value = lax.dynamic_index_in_dim(total, (quad + hop) % quads, 0, keepdims=False)
        part += send(value.astype(BF16), 0, 2 * hop, 0).astype(F32)
    part = part.reshape(2, CORES * feats, half)
    upper = z_place % 2 == 1
    swap = [(i, i ^ CORES) for i in range(groups)]
    part = jnp.where(upper, part[1], part[0]) + lax.ppermute(
        jnp.where(upper, part[0], part[1]), "seq", swap
    )
    part = part.reshape(CORES, feats, half)
    own = jnp.where(odd, part[1], part[0])
    beside = to_core(jnp.where(odd, part[0], part[1]))
    weight_grad = jnp.concatenate([jnp.where(odd, beside, own), jnp.where(odd, own, beside)], 1)
    weight_grad = weight_grad * (rows * groups) ** (-0.5)
    return (query_grad, key_grad, value_grad, weight_grad)


def solution(mesh):
    placed = (P("seq", "ch"),) * 7
    return jax.shard_map(
        shards,
        mesh=mesh,
        in_specs=placed,
        out_specs=(P("seq", "ch"),) * 4,
        check_vma=False,
    )
```

```python
import functools

import jax
import jax.numpy as jnp
import numpy as np
from jax import lax
from jax.experimental import pallas as pl
from jax.experimental.pallas import tpu as pltpu
from jax.sharding import PartitionSpec as P

BF16 = jnp.bfloat16
F32 = jnp.float32

CORES = 2
ALONG_X = 4


def dft_tables(blocks, rows, kept):
    period = 2 * blocks
    length = period * rows
    k1 = np.arange(kept)[:, None]
    used = k1 <= blocks
    angle = 2 * np.pi * ((k1 * np.arange(blocks)[None]) % period) / period
    first = np.concatenate([used * np.cos(angle), used * -np.sin(angle)], 0)
    weight = used * np.where((k1 == 0) | (k1 == blocks), 1.0, 2.0) / length
    last = np.concatenate([(weight * np.cos(angle)).T, -(weight * np.sin(angle)).T], 1)
    turn = 2 * np.pi * (k1 * np.arange(rows)[None]) / length
    twist = np.stack([np.cos(turn), -np.sin(turn)])
    angle = 2 * np.pi * ((np.arange(rows)[:, None] * np.arange(rows)[None]) % rows) / rows
    cos, sin = np.cos(angle), np.sin(angle)
    second = np.block([[cos, -sin], [sin, cos]])
    return first, twist, second, last


def halves(table):
    high = table.astype(BF16)
    low = (table - high.astype(np.float64)).astype(BF16)
    return high, low


def split(value):
    high = value.astype(BF16)
    return high, (value - high.astype(F32)).astype(BF16)


def dot(a, b):
    return jnp.dot(a, b, preferred_element_type=F32)


def dot3(a, b):
    return dot(a[0], b[0]) + (dot(a[0], b[1]) + dot(a[1], b[0]))


def spectrum(x_ref, first_ref, twist_ref, second_ref, plane, blocks, chans, rows, kept):
    plane[...] = x_ref[...].astype(F32)
    data = jnp.concatenate(
        [plane[pl.ds(c, blocks, stride=chans), :] for c in range(chans)], 1
    ).astype(BF16)
    bins = dot(first_ref[0], data) + dot(first_ref[1], data)
    cos, sin = twist_ref[0], twist_ref[1]
    parts = []
    for c in range(chans):
        re = bins[:kept, c * rows : (c + 1) * rows]
        im = bins[kept:, c * rows : (c + 1) * rows]
        parts.append(jnp.concatenate([re * cos - im * sin, re * sin + im * cos], 1))
    return dot3(split(jnp.concatenate(parts, 0)), (second_ref[0], second_ref[1]))


def filter_kernel(sizes, x_ref, first_ref, twist_ref, second_ref, out_ref, plane):
    out_ref[...] = spectrum(x_ref, first_ref, twist_ref, second_ref, plane, *sizes)


def correlate_kernel(
    sizes, x_ref, filt_ref, first_ref, twist_ref, second_ref, back_ref, last_ref, out_ref, plane
):
    blocks, chans, rows, kept = sizes
    grads = spectrum(x_ref, first_ref, twist_ref, second_ref, plane, *sizes)
    g_re, g_im = grads[:, :rows], grads[:, rows:]
    f_re, f_im = filt_ref[:, :rows], filt_ref[:, rows:]
    product = jnp.concatenate([g_re * f_re + g_im * f_im, g_im * f_re - g_re * f_im], 1)
    bins = dot3(split(product), (back_ref[0], back_ref[1]))
    cos, sin = twist_ref[0], twist_ref[1]
    parts = []
    for c in range(chans):
        re = bins[c * kept : (c + 1) * kept, :rows]
        im = bins[c * kept : (c + 1) * kept, rows:]
        parts.append(jnp.concatenate([re * cos + im * sin, im * cos - re * sin], 0))
    inner = dot3((last_ref[0], last_ref[1]), split(jnp.concatenate(parts, 1)))
    for c in range(chans):
        plane[pl.ds(c, blocks, stride=chans), :] = inner[:, c * rows : (c + 1) * rows]
    out_ref[...] = plane[...].astype(BF16)


def pack_kernel(filters_ref, weight_ref, out_ref):
    groups, _, rows = out_ref.shape
    chan = filters_ref.shape[1]
    chans = chan // groups
    feats = weight_ref.shape[0]
    part = chan // (ALONG_X * CORES)
    turned = filters_ref[...].astype(F32).T.astype(BF16)
    out_ref[:, feats // 2 :, :] = turned.reshape(groups, chans, rows)
    weight = weight_ref[...].astype(F32)
    for x in range(ALONG_X):
        for core in range(CORES):
            start = (core * ALONG_X + x) * part
            piece = weight[:, start : start + part]
            folded = jnp.concatenate([piece[: feats // 2], piece[feats // 2 :]], 1).astype(BF16)
            for dest in range(x * groups // ALONG_X + core, (x + 1) * groups // ALONG_X, CORES):
                out_ref[dest, : feats // 2, :] = folded


def gate_kernel(x_ref, left_ref, w0_ref, w1_ref, w2_ref, w3_ref, mine_ref, theirs_ref):
    folded = jnp.concatenate([w0_ref[...], w1_ref[...], w2_ref[...], w3_ref[...]], 1)
    depth = folded.shape[0]
    low = dot(left_ref[:, :depth], folded)
    high = dot(left_ref[:, depth:], folded)
    rows, half = mine_ref.shape
    part = half // ALONG_X
    pieces = [
        low[:, 2 * hop * part : (2 * hop + 1) * part]
        + high[:, (2 * hop + 1) * part : (2 * hop + 2) * part]
        for hop in range(ALONG_X)
    ]
    placed = []
    for x in range(ALONG_X):
        away = (x_ref[0] - x + ALONG_X) % ALONG_X
        value = pieces[0]
        for hop in range(1, ALONG_X):
            value = jnp.where(away == hop, pieces[hop], value)
        placed.append(value)
    share = jnp.concatenate(placed, 1)
    mine_ref[...] = share[:rows]
    theirs_ref[...] = share[rows:]


def grads_kernel(odd_ref, mine_ref, theirs_ref, queries_ref, conv_ref, query_grad_ref, turned_ref):
    odd = odd_ref[0] == 1
    mine, theirs = mine_ref[...], theirs_ref[...]
    gate = jnp.concatenate([jnp.where(odd, theirs, mine), jnp.where(odd, mine, theirs)], 1)
    query_grad_ref[...] = (gate * conv_ref[...].astype(F32)).astype(BF16)
    conv_grad = (gate * queries_ref[...].astype(F32)).astype(BF16)
    turned_ref[...] = conv_grad.astype(F32).T.astype(BF16)


def outputs_kernel(inner_ref, key_ref, value_ref, key_grad_ref, value_grad_ref):
    inner = inner_ref[...].astype(F32).T
    key_grad_ref[...] = (inner * value_ref[...].astype(F32)).astype(BF16)
    value_grad_ref[...] = (inner * key_ref[...].astype(F32)).astype(BF16)


def arrange_kernel(y_ref, *refs):
    block = refs[0].shape[0]
    for hop, ref in enumerate(refs[:-1]):
        start = pl.multiple_of(lax.rem(y_ref[0] + hop, len(refs) - 1) * block, block)
        refs[-1][pl.ds(start, block), :] = ref[...]


def partial_kernel(quad_ref, after_ref, grads_ref, both_ref, own_ref, *away_refs):
    quads = len(away_refs) + 1
    size = grads_ref.shape[0] // (ALONG_X * quads)
    for hop, out_ref in enumerate((own_ref, *away_refs)):
        quad = lax.rem(quad_ref[0] + hop, quads)
        for x in range(ALONG_X):
            start = pl.multiple_of((x * quads + quad) * size, size)
            value = dot(grads_ref[pl.ds(start, size), :], both_ref[...])
            out_ref[x * size : (x + 1) * size, :] = value.astype(out_ref.dtype)


def pairs_kernel(upper_ref, after_ref, own_ref, a_ref, b_ref, c_ref, keep_ref, give_ref):
    total = own_ref[...] + a_ref[...].astype(F32) + b_ref[...].astype(F32) + c_ref[...].astype(F32)
    size = keep_ref.shape[0] // ALONG_X
    upper = upper_ref[0] == 1
    for x in range(ALONG_X):
        low = total[2 * x * size : (2 * x + 1) * size]
        high = total[(2 * x + 1) * size : (2 * x + 2) * size]
        keep_ref[x * size : (x + 1) * size, :] = jnp.where(upper, high, low)
        give_ref[x * size : (x + 1) * size, :] = jnp.where(upper, low, high)


def lines_kernel(x_ref, after_ref, keep_ref, came_ref, *out_refs):
    size = out_refs[0].shape[0]
    for hop, out_ref in enumerate(out_refs):
        place = pl.ds(pl.multiple_of(lax.rem(x_ref[0] + hop, ALONG_X) * size, size), size)
        out_ref[...] = keep_ref[place, :] + came_ref[place, :]


def cores_kernel(odd_ref, own_ref, a_ref, b_ref, c_ref, keep_ref, give_ref):
    total = (own_ref[...] + a_ref[...]) + (b_ref[...] + c_ref[...])
    size = keep_ref.shape[0]
    odd = odd_ref[0] == 1
    keep_ref[...] = jnp.where(odd, total[size:], total[:size])
    give_ref[...] = jnp.where(odd, total[:size], total[size:])


def in_vmem(count):
    return [pl.BlockSpec(memory_space=pltpu.VMEM)] * count


def call(kernel, out, scalars, *operands, scratch=(), after=()):
    return pl.pallas_call(
        kernel,
        out_shape=[jax.ShapeDtypeStruct(shape, dtype) for shape, dtype in out],
        in_specs=[pl.BlockSpec(memory_space=pltpu.SMEM)] * len(scalars)
        + [pl.BlockSpec(memory_space=pl.ANY)] * len(after)
        + in_vmem(len(operands)),
        out_specs=in_vmem(len(out)),
        scratch_shapes=[pltpu.VMEM(shape, F32) for shape in scratch],
        compiler_params=pltpu.CompilerParams(vmem_limit_bytes=32 << 20),
    )(*scalars, *after, *operands)


def shards(queries, key_proj, value_proj, conv_out, filters, out_grad, out_weight):
    rows, chan = queries.shape
    groups = lax.axis_size("seq")
    feats = out_weight.shape[0]
    chips = groups // CORES
    along_z = chips // ALONG_X
    half = chan // CORES
    chans = chan // groups
    kept = -(-(groups + 1) // 8) * 8
    sizes = (groups, chans, rows, kept)

    place = lax.axis_index("seq")
    odd = place % CORES == 1
    x_place = place // (along_z * CORES)
    z_place = place // CORES % along_z
    x_scalar = x_place.reshape(1)
    odd_scalar = odd.astype(jnp.int32).reshape(1)

    def send(value, dx, dz, core):
        pairs = []
        for i in range(groups):
            x, z, c = i // (along_z * CORES), i // CORES % along_z, i % CORES
            x, z, c = (x + dx) % ALONG_X, (z + dz) % along_z, c ^ core
            pairs.append((i, (x * along_z + z) * CORES + c))
        return lax.ppermute(value, "seq", pairs)

    def to_core(value):
        return send(value, 0, 0, 1)

    first, twist, second, last = dft_tables(groups, rows, kept)
    first, last = jnp.stack(halves(first)), jnp.stack(halves(last))
    second, back = jnp.stack(halves(second)), jnp.stack(halves(second.T))
    twist = jnp.asarray(twist, F32)

    def exchange(blocks):
        return lax.all_to_all(blocks.reshape(groups, chans, rows), "seq", 0, 0).reshape(chan, rows)

    (packed,) = call(pack_kernel, [((groups, feats // 2 + chans, rows), BF16)], (), filters, out_weight)
    arrived = lax.all_to_all(packed, "seq", 0, 0)
    folded = arrived[:, : feats // 2].reshape(groups * feats // 2, rows)
    weights = [folded] + [send(folded, hop, 0, 0) for hop in range(1, ALONG_X)]
    (filt,) = call(
        functools.partial(filter_kernel, sizes),
        [((chans * kept, 2 * rows), F32)],
        (),
        arrived[:, feats // 2 :].reshape(chan, rows),
        first,
        twist,
        second,
        scratch=[(chan, rows)],
    )

    features = lax.axis_size("ch")
    turned_grad = out_grad.T
    around = [turned_grad] + [
        lax.ppermute(turned_grad, "ch", [(i, (i - hop) % features) for i in range(features)])
        for hop in range(1, features)
    ]
    (wide,) = call(
        arrange_kernel,
        [((groups * feats, rows), BF16)],
        (lax.axis_index("ch").reshape(1),),
        *around,
    )
    grads = jnp.concatenate([wide, to_core(wide)], 1)
    left = grads.reshape(groups, 2, feats // 2, CORES * rows).transpose(3, 1, 0, 2)

    mine, theirs = call(
        gate_kernel,
        [((rows, half), F32)] * 2,
        (x_scalar,),
        left.reshape(CORES * rows, groups * feats),
        *weights,
    )
    query_grad, turned = call(
        grads_kernel,
        [((rows, chan), BF16), ((chan, rows), BF16)],
        (odd_scalar,),
        mine,
        to_core(theirs),
        queries,
        conv_out,
    )
    (inner,) = call(
        functools.partial(correlate_kernel, sizes),
        [((chan, rows), BF16)],
        (),
        exchange(turned),
        filt,
        first,
        twist,
        second,
        back,
        last,
        scratch=[(chan, rows)],
    )
    key_grad, value_grad = call(
        outputs_kernel, [((rows, chan), BF16)] * 2, (), exchange(inner), key_proj, value_proj
    )

    gated = (queries.astype(F32) * conv_out.astype(F32)).astype(BF16)
    own_half = jnp.where(odd, gated[:, half:], gated[:, :half])
    other_half = jnp.where(odd, gated[:, :half], gated[:, half:])
    both = jnp.concatenate([own_half, to_core(other_half)], 0)
    quads = along_z // 2
    size = groups * feats // quads
    own, *away = call(
        partial_kernel,
        [((size, half), F32)] + [((size, half), BF16)] * (quads - 1),
        ((z_place // 2).reshape(1),),
        grads,
        both,
        after=(arrived,),
    )
    away = [send(value, 0, 2 * hop, 0) for hop, value in enumerate(away, 1)]
    keep, give = call(
        pairs_kernel,
        [((size // 2, half), F32)] * 2,
        ((z_place % 2).reshape(1),),
        own,
        *away,
        after=(turned,),
    )
    swap = [(i, i ^ CORES) for i in range(groups)]
    own, *away = call(
        lines_kernel,
        [((CORES * feats, half), F32)] * ALONG_X,
        (x_scalar,),
        keep,
        lax.ppermute(give, "seq", swap),
        after=(inner,),
    )
    away = [send(value, hop, 0, 0) for hop, value in enumerate(away, 1)]
    keep, give = call(cores_kernel, [((feats, half), F32)] * 2, (odd_scalar,), own, *away)
    give = to_core(give)
    weight_grad = jnp.concatenate([jnp.where(odd, give, keep), jnp.where(odd, keep, give)], 1)
    weight_grad = weight_grad * (rows * groups) ** (-0.5)
    return (query_grad, key_grad, value_grad, weight_grad)


def solution(mesh):
    placed = (P("seq", "ch"),) * 7
    return jax.shard_map(
        shards,
        mesh=mesh,
        in_specs=placed,
        out_specs=(P("seq", "ch"),) * 4,
        check_vma=False,
    )
```

```python
import functools

import jax
import jax.numpy as jnp
import numpy as np
from jax import lax
from jax.experimental import pallas as pl
from jax.experimental.pallas import tpu as pltpu
from jax.sharding import PartitionSpec as P

BF16 = jnp.bfloat16
F32 = jnp.float32

CORES = 2
ALONG_X = 4
CHIPS = 32


def dft_tables(blocks, rows, kept):
    period = 2 * blocks
    length = period * rows
    k1 = np.arange(kept)[:, None]
    used = k1 <= blocks
    angle = 2 * np.pi * ((k1 * np.arange(blocks)[None]) % period) / period
    first = np.concatenate([used * np.cos(angle), used * -np.sin(angle)], 0)
    weight = used * np.where((k1 == 0) | (k1 == blocks), 1.0, 2.0) / length
    last = np.concatenate([(weight * np.cos(angle)).T, -(weight * np.sin(angle)).T], 1)
    turn = 2 * np.pi * (k1 * np.arange(rows)[None]) / length
    twist = np.stack([np.cos(turn), -np.sin(turn)])
    angle = 2 * np.pi * ((np.arange(rows)[:, None] * np.arange(rows)[None]) % rows) / rows
    cos, sin = np.cos(angle), np.sin(angle)
    second = np.block([[cos, -sin], [sin, cos]])
    return first, twist, second, last


def halves(table):
    high = table.astype(BF16)
    low = (table - high.astype(np.float64)).astype(BF16)
    return high, low


def split(value):
    high = value.astype(BF16)
    return high, (value - high.astype(F32)).astype(BF16)


def dot(a, b):
    return jnp.dot(a, b, preferred_element_type=F32)


def dot3(a, b):
    return dot(a[0], b[0]) + (dot(a[0], b[1]) + dot(a[1], b[0]))


def spectrum(data, first_ref, twist_ref, second_ref, chans, rows, kept):
    bins = dot(first_ref[0], data) + dot(first_ref[1], data)
    cos, sin = twist_ref[0], twist_ref[1]
    parts = []
    for c in range(chans):
        re = bins[:kept, c * rows : (c + 1) * rows]
        im = bins[kept:, c * rows : (c + 1) * rows]
        parts.append(jnp.concatenate([re * cos - im * sin, re * sin + im * cos], 1))
    return dot3(split(jnp.concatenate(parts, 0)), (second_ref[0], second_ref[1]))


def filter_kernel(sizes, x_ref, first_ref, twist_ref, second_ref, out_ref, plane):
    chips, chans, rows, kept = sizes
    plane[...] = x_ref[...].astype(F32)
    data = jnp.concatenate(
        [
            jnp.concatenate(
                [
                    plane[pl.ds(core * chans + c, chips, stride=CORES * chans), :]
                    for core in range(CORES)
                ],
                0,
            )
            for c in range(chans)
        ],
        1,
    ).astype(BF16)
    out_ref[...] = spectrum(data, first_ref, twist_ref, second_ref, chans, rows, kept)


def correlate_kernel(sizes, *refs):
    x_ref, filt_ref, first_ref, twist_ref, second_ref, back_ref, last_ref = refs[:7]
    kept_ref, *came_refs, out_ref, wide, plane = refs[7:]
    chips, chans, rows, kept = sizes
    for core in range(CORES):
        wide[core] = x_ref[:, core * rows : (core + 1) * rows].astype(F32)
    data = jnp.concatenate(
        [
            jnp.concatenate(
                [wide[core, pl.ds(c, chips, stride=chans), :] for core in range(CORES)], 0
            )
            for c in range(chans)
        ],
        1,
    ).astype(BF16)
    grads = spectrum(data, first_ref, twist_ref, second_ref, chans, rows, kept)
    g_re, g_im = grads[:, :rows], grads[:, rows:]
    f_re, f_im = filt_ref[:, :rows], filt_ref[:, rows:]
    product = jnp.concatenate([g_re * f_re + g_im * f_im, g_im * f_re - g_re * f_im], 1)
    bins = dot3(split(product), (back_ref[0], back_ref[1]))
    cos, sin = twist_ref[0], twist_ref[1]
    parts = []
    for c in range(chans):
        re = bins[c * kept : (c + 1) * kept, :rows]
        im = bins[c * kept : (c + 1) * kept, rows:]
        parts.append(jnp.concatenate([re * cos + im * sin, im * cos - re * sin], 0))
    inner = dot3((last_ref[0], last_ref[1]), split(jnp.concatenate(parts, 1)))
    for c in range(chans):
        for core in range(CORES):
            plane[pl.ds(core * chans + c, chips, stride=CORES * chans), :] = inner[
                core * chips : (core + 1) * chips, c * rows : (c + 1) * rows
            ]
    groups, depth, _ = out_ref.shape
    came = jnp.concatenate([ref[...] for ref in came_refs], 0)
    total = (kept_ref[...] + came.astype(F32)).astype(BF16)
    out_ref[:, : depth - chans, :] = total.reshape(groups, depth - chans, rows)
    out_ref[:, depth - chans :, :] = plane[...].astype(BF16).reshape(groups, chans, rows)


def pack_kernel(filters_ref, weight_ref, out_ref):
    groups, _, rows = out_ref.shape
    chan = filters_ref.shape[1]
    chans = chan // groups
    feats = weight_ref.shape[0]
    part = chan // (ALONG_X * CORES)
    turned = filters_ref[...].astype(F32).T.reshape(CORES, groups // CORES, chans, rows)
    turned = jnp.swapaxes(turned, 0, 1).reshape(groups, chans, rows)
    out_ref[:, feats // 2 :, :] = turned.astype(BF16)
    weight = weight_ref[...].astype(F32)
    for x in range(ALONG_X):
        for core in range(CORES):
            start = (core * ALONG_X + x) * part
            piece = weight[:, start : start + part]
            folded = jnp.concatenate([piece[: feats // 2], piece[feats // 2 :]], 1).astype(BF16)
            for dest in range(x * groups // ALONG_X + core, (x + 1) * groups // ALONG_X, CORES):
                out_ref[dest, : feats // 2, :] = folded


def left_kernel(mine_ref, theirs_ref, out_ref):
    rows = mine_ref.shape[1]
    depth = mine_ref.shape[0] // 2
    for i, ref in enumerate((mine_ref, theirs_ref)):
        turned = ref[...].reshape(2 * CHIPS, 2, depth // (2 * CHIPS), rows)
        for part in range(2):
            value = turned[:, part].reshape(depth, rows).astype(F32).T
            out_ref[i * rows : (i + 1) * rows, part * depth : (part + 1) * depth] = value.astype(BF16)


def halves_kernel(odd_ref, *refs):
    queries_ref, conv_ref, own_ref, other_ref = refs[-4:]
    odd = odd_ref[0] == 1
    rows, half = queries_ref.shape[0], own_ref.shape[1]
    for i, ref in enumerate((queries_ref, conv_ref)):
        left, right = ref[:, :half], ref[:, half:]
        own_ref[i * rows : (i + 1) * rows, :] = jnp.where(odd, right, left)
        other_ref[i * rows : (i + 1) * rows, :] = jnp.where(odd, left, right)


def both_cores(own_ref, came_ref):
    rows = own_ref.shape[0] // 2
    own, came = own_ref[...].astype(F32), came_ref[...].astype(F32)
    return (
        jnp.concatenate([own[:rows], came[:rows]], 0),
        jnp.concatenate([own[rows:], came[rows:]], 0),
    )


def gate_kernel(x_ref, odd_ref, *refs):
    own_ref, came_ref, left_ref, w0_ref, w1_ref, w2_ref, w3_ref, turned_ref, mine_ref, theirs_ref = refs[-10:]
    odd = odd_ref[0] == 1
    folded = jnp.concatenate([w0_ref[...], w1_ref[...], w2_ref[...], w3_ref[...]], 1)
    depth = folded.shape[0]
    low = dot(left_ref[:, :depth], folded)
    high = dot(left_ref[:, depth:], folded)
    rows, half = mine_ref.shape
    part = half // ALONG_X
    pieces = [
        low[:, 2 * hop * part : (2 * hop + 1) * part]
        + high[:, (2 * hop + 1) * part : (2 * hop + 2) * part]
        for hop in range(ALONG_X)
    ]
    placed = []
    for x in range(ALONG_X):
        away = (x_ref[0] - x + ALONG_X) % ALONG_X
        value = pieces[0]
        for hop in range(1, ALONG_X):
            value = jnp.where(away == hop, pieces[hop], value)
        placed.append(value)
    gate = jnp.concatenate(placed, 1)
    queries, conv = both_cores(own_ref, came_ref)
    turned = (gate * queries).astype(BF16).astype(F32).T
    swapped = jnp.concatenate([turned[:, rows:], turned[:, :rows]], 1)
    turned_ref[...] = jnp.where(odd, swapped, turned).astype(BF16)
    query_grad = (gate * conv).astype(BF16)
    mine_ref[...] = query_grad[:rows]
    theirs_ref[...] = query_grad[rows:]


def outputs_kernel(scale, came_ref, key_ref, value_ref, key_grad_ref, value_grad_ref, weight_grad_ref):
    rows, chan = key_ref.shape
    groups, depth, _ = came_ref.shape
    feats, chans = weight_grad_ref.shape[0], chan // groups
    folded = feats // 2
    inner = came_ref[:, folded:, :].astype(F32).reshape(CHIPS, CORES, chans, rows)
    inner = jnp.swapaxes(inner, 0, 1).reshape(chan, rows).T
    key_grad_ref[...] = (inner * value_ref[...].astype(F32)).astype(BF16)
    value_grad_ref[...] = (inner * key_ref[...].astype(F32)).astype(BF16)
    sums = came_ref[:, :folded, :].astype(F32)
    sums = sums.reshape(ALONG_X // 2, 2, CHIPS // ALONG_X // 2, 2, CORES, folded, rows)
    sums = jnp.sum(jnp.sum(sums, 2), 0) * scale
    part = rows // 2
    for high in range(2):
        value = jnp.concatenate(
            [
                sums[x, z, core, :, high * part : (high + 1) * part]
                for core in range(CORES)
                for z in range(2)
                for x in range(2)
            ],
            1,
        )
        weight_grad_ref[high * folded : (high + 1) * folded, :] = value


def arrange_kernel(y_ref, after_ref, *refs):
    block = refs[0].shape[0]
    for hop, ref in enumerate(refs[:-1]):
        start = pl.multiple_of(lax.rem(y_ref[0] + hop, len(refs) - 1) * block, block)
        refs[-1][pl.ds(start, block), :] = ref[...]


def partial_kernel(upper_ref, mine_ref, theirs_ref, own_ref, came_ref, keep_ref, *give_refs):
    queries, conv = both_cores(own_ref, came_ref)
    gated = (queries * conv).astype(BF16)
    part = gated.shape[1] // 2
    upper = upper_ref[0] == 1
    low, high = gated[:, :part], gated[:, part:]
    left = jnp.concatenate([mine_ref[...], theirs_ref[...]], 1)
    keep_ref[...] = dot(left, jnp.where(upper, high, low))
    give = dot(left, jnp.where(upper, low, high)).astype(BF16)
    size = give_refs[0].shape[0]
    for i, ref in enumerate(give_refs):
        ref[...] = give[i * size : (i + 1) * size]


def fold_kernel(upper_ref, after_ref, keep_ref, low_ref, high_ref, kept_ref, *give_refs):
    total = keep_ref[...] + jnp.concatenate([low_ref[...], high_ref[...]], 0).astype(F32)
    depth, width = total.shape
    total = total.reshape(CORES * CHIPS, 2, depth // (2 * CORES * CHIPS), width)
    first = total[:, 0].reshape(depth // 2, width)
    second = total[:, 1].reshape(depth // 2, width)
    part = width // 2
    low = jnp.concatenate([first[:, :part], second[:, :part]], 1)
    high = jnp.concatenate([first[:, part:], second[:, part:]], 1)
    upper = upper_ref[0] == 1
    kept_ref[...] = jnp.where(upper, high, low)
    give = jnp.where(upper, low, high).astype(BF16)
    size = give_refs[0].shape[0]
    for i, ref in enumerate(give_refs):
        ref[...] = give[i * size : (i + 1) * size]


def in_vmem(count):
    return [pl.BlockSpec(memory_space=pltpu.VMEM)] * count


def call(kernel, out, scalars, *operands, scratch=(), after=()):
    return pl.pallas_call(
        kernel,
        out_shape=[jax.ShapeDtypeStruct(shape, dtype) for shape, dtype in out],
        in_specs=[pl.BlockSpec(memory_space=pltpu.SMEM)] * len(scalars)
        + [pl.BlockSpec(memory_space=pl.ANY)] * len(after)
        + in_vmem(len(operands)),
        out_specs=in_vmem(len(out)),
        scratch_shapes=[pltpu.VMEM(shape, F32) for shape in scratch],
        compiler_params=pltpu.CompilerParams(vmem_limit_bytes=10 << 20),
    )(*scalars, *after, *operands)


def shards(queries, key_proj, value_proj, conv_out, filters, out_grad, out_weight):
    rows, chan = queries.shape
    groups = lax.axis_size("seq")
    feats = out_weight.shape[0]
    chips = groups // CORES
    along_z = chips // ALONG_X
    half = chan // CORES
    chans = chan // groups
    kept = -(-(groups + 1) // 8) * 8
    sizes = (chips, chans, rows, kept)

    place = lax.axis_index("seq")
    odd = place % CORES == 1
    x_place = place // (along_z * CORES)
    z_place = place // CORES % along_z
    x_scalar = x_place.reshape(1)
    odd_scalar = odd.astype(jnp.int32).reshape(1)

    def send(value, dx, dz, core):
        pairs = []
        for i in range(groups):
            x, z, c = i // (along_z * CORES), i // CORES % along_z, i % CORES
            x, z, c = (x + dx) % ALONG_X, (z + dz) % along_z, c ^ core
            pairs.append((i, (x * along_z + z) * CORES + c))
        return lax.ppermute(value, "seq", pairs)

    def to_core(value):
        return send(value, 0, 0, 1)

    order = np.arange(groups).reshape(chips, CORES).T.reshape(-1)
    first, twist, second, last = dft_tables(groups, rows, kept)
    first, last = first[:, order], last[order]
    first, last = jnp.stack(halves(first)), jnp.stack(halves(last))
    second, back = jnp.stack(halves(second)), jnp.stack(halves(second.T))
    twist = jnp.asarray(twist, F32)

    def by_core(own, other):
        return jnp.concatenate([jnp.where(odd, other, own), jnp.where(odd, own, other)], 1)

    (packed,) = call(pack_kernel, [((groups, feats // 2 + chans, rows), BF16)], (), filters, out_weight)
    arrived = lax.all_to_all(packed, "seq", 0, 0)
    folded = arrived[:, : feats // 2].reshape(groups * feats // 2, rows)
    weights = [folded] + [send(folded, hop, 0, 0) for hop in range(1, ALONG_X)]
    (filt,) = call(
        functools.partial(filter_kernel, sizes),
        [((chans * kept, 2 * rows), F32)],
        (),
        arrived[:, feats // 2 :].reshape(chan, rows),
        first,
        twist,
        second,
        scratch=[(chan, rows)],
    )

    features = lax.axis_size("ch")
    turned_grad = out_grad.T
    around = [turned_grad] + [
        lax.ppermute(turned_grad, "ch", [(i, (i - hop) % features) for i in range(features)])
        for hop in range(1, features)
    ]
    (wide,) = call(
        arrange_kernel,
        [((groups * feats, rows), BF16)],
        (lax.axis_index("ch").reshape(1),),
        *around,
        after=(arrived,),
    )
    wide_there = to_core(wide)
    (left,) = call(
        left_kernel, [((CORES * rows, groups * feats), BF16)], (), wide, wide_there
    )
    halves_own, halves_other = call(
        halves_kernel, [((CORES * rows, half), BF16)] * 2, (odd_scalar,), queries, conv_out
    )
    halves_came = to_core(halves_other)

    keep, *give = call(
        partial_kernel,
        [((groups * feats, half // 2), F32)] + [((groups * feats // 2, half // 2), BF16)] * 2,
        ((z_place % 2).reshape(1),),
        wide,
        wide_there,
        halves_own,
        halves_came,
    )
    turned, mine, theirs = call(
        gate_kernel,
        [((half, CORES * rows), BF16)] + [((rows, half), BF16)] * 2,
        (x_scalar, odd_scalar),
        halves_own,
        halves_came,
        left,
        *weights,
        after=(filt,),
    )
    keep, *give = call(
        fold_kernel,
        [((groups * feats // 2, half // 2), F32)]
        + [((groups * feats // 4, half // 2), BF16)] * 2,
        ((x_place % 2).reshape(1),),
        keep,
        *[lax.ppermute(value, "seq", [(i, i ^ CORES) for i in range(groups)]) for value in give],
        after=(turned,),
    )
    came = [
        lax.ppermute(value, "seq", [(i, i ^ (along_z * CORES)) for i in range(groups)])
        for value in give
    ]

    received = lax.all_to_all(
        turned.reshape(chips, chans, CORES * rows),
        "seq",
        0,
        0,
        axis_index_groups=[list(range(core, groups, CORES)) for core in range(CORES)],
    )
    query_grad = by_core(mine, to_core(theirs))
    (inner,) = call(
        functools.partial(correlate_kernel, sizes),
        [((groups, feats // 2 + chans, rows), BF16)],
        (),
        received.reshape(half, CORES * rows),
        filt,
        first,
        twist,
        second,
        back,
        last,
        keep,
        *came,
        scratch=[(CORES, half, rows), (chan, rows)],
    )
    key_grad, value_grad, weight_grad = call(
        functools.partial(outputs_kernel, (rows * groups) ** (-0.5)),
        [((rows, chan), BF16)] * 2 + [((feats, chan), F32)],
        (),
        lax.all_to_all(inner, "seq", 0, 0),
        key_proj,
        value_proj,
    )
    return (query_grad, key_grad, value_grad, weight_grad)


def solution(mesh):
    placed = (P("seq", "ch"),) * 7
    return jax.shard_map(
        shards,
        mesh=mesh,
        in_specs=placed,
        out_specs=(P("seq", "ch"),) * 4,
        check_vma=False,
    )
```

```python
import functools

import jax
import jax.numpy as jnp
import numpy as np
from jax import lax
from jax.experimental import pallas as pl
from jax.experimental.pallas import tpu as pltpu
from jax.sharding import PartitionSpec as P

BF16 = jnp.bfloat16
F32 = jnp.float32

CORES = 2
ALONG_X = 4
ALONG_Y = 4
CHIPS = 32
ALONG_Z = CHIPS // ALONG_X


def own_place():
    place = lax.axis_index("seq")
    return place // (ALONG_Z * CORES), place // CORES % ALONG_Z, place % CORES


def dft_tables(blocks, rows, kept):
    period = 2 * blocks
    length = period * rows
    k1 = np.arange(kept)[:, None]
    used = k1 <= blocks
    angle = 2 * np.pi * ((k1 * np.arange(blocks)[None]) % period) / period
    first = np.concatenate([used * np.cos(angle), used * -np.sin(angle)], 0)
    weight = used * np.where((k1 == 0) | (k1 == blocks), 1.0, 2.0) / length
    last = np.concatenate([(weight * np.cos(angle)).T, -(weight * np.sin(angle)).T], 1)
    turn = 2 * np.pi * (k1 * np.arange(rows)[None]) / length
    twist = np.stack([np.cos(turn), -np.sin(turn)])
    angle = 2 * np.pi * ((np.arange(rows)[:, None] * np.arange(rows)[None]) % rows) / rows
    cos, sin = np.cos(angle), np.sin(angle)
    second = np.block([[cos, -sin], [sin, cos]])
    return first, twist, second, last


def halves(table):
    high = table.astype(BF16)
    low = (table - high.astype(np.float64)).astype(BF16)
    return high, low


def split(value):
    high = value.astype(BF16)
    return high, (value - high.astype(F32)).astype(BF16)


def dot(a, b):
    return jnp.dot(a, b, preferred_element_type=F32)


def dot3(a, b):
    return dot(a[0], b[0]) + (dot(a[0], b[1]) + dot(a[1], b[0]))


def spectrum(data, first_ref, twist_ref, second_ref, chans, rows, kept):
    bins = dot(first_ref[0], data) + dot(first_ref[1], data)
    cos, sin = twist_ref[0], twist_ref[1]
    parts = []
    for c in range(chans):
        re = bins[:kept, c * rows : (c + 1) * rows]
        im = bins[kept:, c * rows : (c + 1) * rows]
        parts.append(jnp.concatenate([re * cos - im * sin, re * sin + im * cos], 1))
    return dot3(split(jnp.concatenate(parts, 0)), (second_ref[0], second_ref[1]))


def by_channel(planes, chips, chans):
    return jnp.concatenate(
        [
            jnp.concatenate(
                [planes[core, pl.ds(c, chips, stride=chans), :] for core in range(CORES)], 0
            )
            for c in range(chans)
        ],
        1,
    ).astype(BF16)


def filter_kernel(sizes, own_ref, came_ref, first_ref, twist_ref, second_ref, out_ref, planes):
    chips, chans, rows, kept = sizes
    odd = own_place()[2] == 1
    own, came = own_ref[...].astype(F32), came_ref[...].astype(F32)
    planes[0] = jnp.where(odd, came, own)
    planes[1] = jnp.where(odd, own, came)
    data = by_channel(planes, chips, chans)
    out_ref[...] = spectrum(data, first_ref, twist_ref, second_ref, chans, rows, kept)


def correlate_kernel(sizes, *refs):
    x_ref, filt_ref, first_ref, twist_ref, second_ref, back_ref, last_ref = refs[1:8]
    kept_ref, *came_refs, out_ref, wide, plane = refs[8:]
    chips, chans, rows, kept = sizes
    for core in range(CORES):
        wide[core] = x_ref[:, core * rows : (core + 1) * rows].astype(F32)
    data = by_channel(wide, chips, chans)
    grads = spectrum(data, first_ref, twist_ref, second_ref, chans, rows, kept)
    g_re, g_im = grads[:, :rows], grads[:, rows:]
    f_re, f_im = filt_ref[:, :rows], filt_ref[:, rows:]
    product = jnp.concatenate([g_re * f_re + g_im * f_im, g_im * f_re - g_re * f_im], 1)
    bins = dot3(split(product), (back_ref[0], back_ref[1]))
    cos, sin = twist_ref[0], twist_ref[1]
    parts = []
    for c in range(chans):
        re = bins[c * kept : (c + 1) * kept, :rows]
        im = bins[c * kept : (c + 1) * kept, rows:]
        parts.append(jnp.concatenate([re * cos + im * sin, im * cos - re * sin], 0))
    inner = dot3((last_ref[0], last_ref[1]), split(jnp.concatenate(parts, 1)))
    for c in range(chans):
        for core in range(CORES):
            plane[pl.ds(core * chans + c, chips, stride=CORES * chans), :] = inner[
                core * chips : (core + 1) * chips, c * rows : (c + 1) * rows
            ]
    groups, depth, _ = out_ref.shape
    came = jnp.concatenate([ref[...] for ref in came_refs], 0)
    total = (kept_ref[...] + came.astype(F32)).astype(BF16)
    out_ref[:, : depth - chans, :] = total.reshape(groups, depth - chans, rows)
    out_ref[:, depth - chans :, :] = plane[...].astype(BF16).reshape(groups, chans, rows)


def pack_kernel(filters_ref, weight_ref, out_ref):
    chips, depth, rows = out_ref.shape
    chan = filters_ref.shape[1]
    feats = weight_ref.shape[0]
    turned = filters_ref[...].astype(F32).T.reshape(CORES, chips, chan // (CORES * chips), rows)
    turned = jnp.swapaxes(turned, 0, 1).reshape(chips, depth - CORES * feats, rows)
    out_ref[:, CORES * feats :, :] = turned.astype(BF16)
    for core in range(CORES):
        for part in range(2):
            start = (core * 2 + part) * rows
            piece = weight_ref[:, start : start + rows]
            for chip in range(chips):
                if chip // ALONG_Z % 2 == part:
                    out_ref[chip, core * feats : (core + 1) * feats, :] = piece


def unpack_kernel(came_ref, own_ref, other_ref):
    feats = own_ref.shape[0] // CHIPS
    odd = own_place()[2] == 1
    first, second = came_ref[:, :feats, :], came_ref[:, feats : 2 * feats, :]
    own_ref[...] = jnp.where(odd, second, first).reshape(own_ref.shape)
    other_ref[...] = jnp.where(odd, first, second).reshape(other_ref.shape)


def unpack_filters_kernel(came_ref, own_ref, other_ref):
    chans = own_ref.shape[0] // CHIPS
    odd = own_place()[2] == 1
    came = came_ref[:, -CORES * chans :, :].astype(F32)
    came = came.reshape(CHIPS, CORES, chans, came.shape[2])
    first, second = came[:, 0], came[:, 1]
    own_ref[...] = jnp.where(odd, second, first).reshape(own_ref.shape).astype(BF16)
    other_ref[...] = jnp.where(odd, first, second).reshape(other_ref.shape).astype(BF16)


def left_kernel(mine_ref, theirs_ref, out_ref):
    depth, rows = mine_ref.shape[0] // CORES, mine_ref.shape[1]
    odd = own_place()[2] == 1
    for i, ref in enumerate((mine_ref, theirs_ref)):
        value = ref[...].reshape(CHIPS, CORES, depth // CHIPS, rows)
        first, second = (value[:, core].reshape(depth, rows).astype(F32) for core in range(CORES))
        place = slice(i * rows, (i + 1) * rows)
        out_ref[place, :depth] = jnp.where(odd, second, first).T.astype(BF16)
        out_ref[place, depth:] = jnp.where(odd, first, second).T.astype(BF16)


def halves_kernel(*refs):
    queries_ref, conv_ref, own_ref, other_ref = refs[-4:]
    odd = own_place()[2] == 1
    rows, half = queries_ref.shape[0], own_ref.shape[1]
    for i, ref in enumerate((queries_ref, conv_ref)):
        left, right = ref[:, :half], ref[:, half:]
        own_ref[i * rows : (i + 1) * rows, :] = jnp.where(odd, right, left)
        other_ref[i * rows : (i + 1) * rows, :] = jnp.where(odd, left, right)


def both_cores(own_ref, came_ref):
    rows = own_ref.shape[0] // 2
    own, came = own_ref[...].astype(F32), came_ref[...].astype(F32)
    return (
        jnp.concatenate([own[:rows], came[:rows]], 0),
        jnp.concatenate([own[rows:], came[rows:]], 0),
    )


def gate_kernel(*refs):
    own_ref, came_ref, left_ref, a_ref, b_ref, c_ref, d_ref, turned_ref, mine_ref, theirs_ref = refs[-10:]
    x, _, core = own_place()
    odd = core == 1
    rows = mine_ref.shape[0]
    depth = a_ref.shape[0]
    gate = dot(left_ref[:, :depth], jnp.concatenate([a_ref[...], b_ref[...]], 1))
    gate += dot(left_ref[:, depth:], jnp.concatenate([c_ref[...], d_ref[...]], 1))
    part = gate.shape[1] // 2
    gate = jnp.where(x % 2 == 1, jnp.concatenate([gate[:, part:], gate[:, :part]], 1), gate)
    queries, conv = both_cores(own_ref, came_ref)
    turned = (gate * queries).astype(BF16).astype(F32).T
    swapped = jnp.concatenate([turned[:, rows:], turned[:, :rows]], 1)
    turned_ref[...] = jnp.where(odd, swapped, turned).astype(BF16)
    query_grad = (gate * conv).astype(BF16)
    mine_ref[...] = query_grad[:rows]
    theirs_ref[...] = query_grad[rows:]


def join_kernel(mine_ref, theirs_ref, out_ref):
    odd = own_place()[2] == 1
    mine, theirs = mine_ref[...], theirs_ref[...]
    half = mine.shape[1]
    out_ref[:, :half] = jnp.where(odd, theirs, mine)
    out_ref[:, half:] = jnp.where(odd, mine, theirs)


def outputs_kernel(scale, came_ref, key_ref, value_ref, key_grad_ref, value_grad_ref, weight_grad_ref):
    rows, chan = key_ref.shape
    groups, depth, _ = came_ref.shape
    feats, chans = weight_grad_ref.shape[0], chan // groups
    folded = feats // 2
    inner = came_ref[:, folded:, :].astype(F32).reshape(CHIPS, CORES, chans, rows)
    inner = jnp.swapaxes(inner, 0, 1).reshape(chan, rows).T
    key_grad_ref[...] = (inner * value_ref[...].astype(F32)).astype(BF16)
    value_grad_ref[...] = (inner * key_ref[...].astype(F32)).astype(BF16)
    sums = came_ref[:, :folded, :].astype(F32)
    sums = sums.reshape(ALONG_X // 2, 2, CHIPS // ALONG_X // 2, 2, CORES, folded, rows)
    sums = jnp.sum(jnp.sum(sums, 2), 0) * scale
    part = rows // 2
    for high in range(2):
        value = jnp.concatenate(
            [
                sums[x, z, core, :, high * part : (high + 1) * part]
                for core in range(CORES)
                for z in range(2)
                for x in range(2)
            ],
            1,
        )
        weight_grad_ref[high * folded : (high + 1) * folded, :] = value


def arrange_kernel(*refs):
    *block_refs, out_ref = refs[-ALONG_Y - 1 :]
    size = block_refs[0].shape[0]
    for hop, ref in enumerate(block_refs):
        start = pl.multiple_of(lax.rem(lax.axis_index("ch") + hop, ALONG_Y) * size, size)
        out_ref[pl.ds(start, size), :] = ref[...]


def partial_kernel(mine_ref, theirs_ref, own_ref, came_ref, keep_ref, *give_refs):
    queries, conv = both_cores(own_ref, came_ref)
    gated = (queries * conv).astype(BF16)
    part = gated.shape[1] // 2
    upper = own_place()[1] % 2 == 1
    low, high = gated[:, :part], gated[:, part:]
    left = jnp.concatenate([mine_ref[...], theirs_ref[...]], 1)
    keep_ref[...] = dot(left, jnp.where(upper, high, low)).astype(BF16)
    give = dot(left, jnp.where(upper, low, high)).astype(BF16)
    size = give_refs[0].shape[0]
    for i, ref in enumerate(give_refs):
        ref[...] = give[i * size : (i + 1) * size]


def fold_kernel(after_ref, keep_ref, low_ref, high_ref, kept_ref, *give_refs):
    total = keep_ref[...].astype(F32) + jnp.concatenate([low_ref[...], high_ref[...]], 0).astype(F32)
    depth, width = total.shape
    total = total.reshape(CORES * CHIPS, 2, depth // (2 * CORES * CHIPS), width)
    first = total[:, 0].reshape(depth // 2, width)
    second = total[:, 1].reshape(depth // 2, width)
    part = width // 2
    low = jnp.concatenate([first[:, :part], second[:, :part]], 1)
    high = jnp.concatenate([first[:, part:], second[:, part:]], 1)
    upper = own_place()[0] % 2 == 1
    kept_ref[...] = jnp.where(upper, high, low)
    give = jnp.where(upper, low, high).astype(BF16)
    size = give_refs[0].shape[0]
    for i, ref in enumerate(give_refs):
        ref[...] = give[i * size : (i + 1) * size]


def in_vmem(count):
    return [pl.BlockSpec(memory_space=pltpu.VMEM)] * count


def call(kernel, out, *operands, scratch=(), after=()):
    return pl.pallas_call(
        kernel,
        out_shape=[jax.ShapeDtypeStruct(shape, dtype) for shape, dtype in out],
        in_specs=[pl.BlockSpec(memory_space=pl.ANY)] * len(after) + in_vmem(len(operands)),
        out_specs=in_vmem(len(out)),
        scratch_shapes=[pltpu.VMEM(shape, F32) for shape in scratch],
        compiler_params=pltpu.CompilerParams(vmem_limit_bytes=10 << 20),
    )(*after, *operands)


def shards(queries, key_proj, value_proj, conv_out, filters, out_grad, out_weight):
    rows, chan = queries.shape
    groups = lax.axis_size("seq")
    feats = out_weight.shape[0]
    chips = groups // CORES
    along_z = chips // ALONG_X
    half = chan // CORES
    chans = chan // groups
    kept = -(-(groups + 1) // 8) * 8
    sizes = (chips, chans, rows, kept)

    def send(value, dx, dz, core):
        pairs = []
        for i in range(groups):
            x, z, c = i // (along_z * CORES), i // CORES % along_z, i % CORES
            x, z, c = (x + dx) % ALONG_X, (z + dz) % along_z, c ^ core
            pairs.append((i, (x * along_z + z) * CORES + c))
        return lax.ppermute(value, "seq", pairs)

    def to_core(value):
        return send(value, 0, 0, 1)

    order = np.arange(groups).reshape(chips, CORES).T.reshape(-1)
    first, twist, second, last = dft_tables(groups, rows, kept)
    first, last = first[:, order], last[order]
    first, last = jnp.stack(halves(first)), jnp.stack(halves(last))
    second, back = jnp.stack(halves(second)), jnp.stack(halves(second.T))
    twist = jnp.asarray(twist, F32)

    (packed,) = call(
        pack_kernel, [((chips, CORES * (feats + chans), rows), BF16)], filters, out_weight
    )
    like_cores = [list(range(core, groups, CORES)) for core in range(CORES)]
    arrived = lax.all_to_all(packed, "seq", 0, 0, axis_index_groups=like_cores)
    weight_own, weight_other = call(unpack_kernel, [((chips * feats, rows), BF16)] * 2, arrived)
    weight_came = to_core(weight_other)
    weights = [
        weight_own, send(weight_own, 1, 0, 0), weight_came, send(weight_came, -1, 0, 0)
    ]
    filters_own, filters_other = call(
        unpack_filters_kernel, [((chips * chans, rows), BF16)] * 2, arrived
    )
    (filt,) = call(
        functools.partial(filter_kernel, sizes),
        [((chans * kept, 2 * rows), F32)],
        filters_own,
        to_core(filters_other),
        first,
        twist,
        second,
        scratch=[(CORES, half, rows)],
    )

    halves_own, halves_other = call(
        halves_kernel, [((CORES * rows, half), BF16)] * 2, queries, conv_out
    )

    features = lax.axis_size("ch")
    turned_grad = out_grad.T
    around = [turned_grad] + [
        lax.ppermute(turned_grad, "ch", [(i, (i - hop) % features) for i in range(features)])
        for hop in range(1, features)
    ]
    (wide,) = call(
        arrange_kernel,
        [((groups * feats, rows), BF16)],
        *around,
        after=(arrived, halves_own),
    )
    wide_there = to_core(wide)
    (left,) = call(
        left_kernel, [((CORES * rows, groups * feats), BF16)], wide, wide_there
    )
    halves_came = to_core(halves_other)

    keep, *give = call(
        partial_kernel,
        [((groups * feats, half // 2), BF16)] + [((groups * feats // 2, half // 2), BF16)] * 2,
        wide,
        wide_there,
        halves_own,
        halves_came,
    )
    turned, mine, theirs = call(
        gate_kernel,
        [((half, CORES * rows), BF16)] + [((rows, half), BF16)] * 2,
        halves_own,
        halves_came,
        left,
        *weights,
        after=(filt,),
    )
    keep, *give = call(
        fold_kernel,
        [((groups * feats // 2, half // 2), F32)]
        + [((groups * feats // 4, half // 2), BF16)] * 2,
        keep,
        *[lax.ppermute(value, "seq", [(i, i ^ CORES) for i in range(groups)]) for value in give],
        after=(turned,),
    )
    came = [
        lax.ppermute(value, "seq", [(i, i ^ (along_z * CORES)) for i in range(groups)])
        for value in give
    ]

    received = lax.all_to_all(
        turned.reshape(chips, chans, CORES * rows),
        "seq",
        0,
        0,
        axis_index_groups=like_cores,
    )
    theirs = to_core(theirs)
    (query_grad,) = call(join_kernel, [((rows, chan), BF16)], mine, theirs)
    (inner,) = call(
        functools.partial(correlate_kernel, sizes),
        [((groups, feats // 2 + chans, rows), BF16)],
        received.reshape(half, CORES * rows),
        filt,
        first,
        twist,
        second,
        back,
        last,
        keep,
        *came,
        scratch=[(CORES, half, rows), (chan, rows)],
        after=(theirs,),
    )
    key_grad, value_grad, weight_grad = call(
        functools.partial(outputs_kernel, (rows * groups) ** (-0.5)),
        [((rows, chan), BF16)] * 2 + [((feats, chan), F32)],
        lax.all_to_all(inner, "seq", 0, 0),
        key_proj,
        value_proj,
    )
    return (query_grad, key_grad, value_grad, weight_grad)


def solution(mesh):
    placed = (P("seq", "ch"),) * 7
    return jax.shard_map(
        shards,
        mesh=mesh,
        in_specs=placed,
        out_specs=(P("seq", "ch"),) * 4,
        check_vma=False,
    )
```

```python
import functools

import jax
import jax.numpy as jnp
import numpy as np
from jax import lax
from jax.experimental import pallas as pl
from jax.experimental.pallas import tpu as pltpu
from jax.sharding import PartitionSpec as P

BF16 = jnp.bfloat16
F32 = jnp.float32

CORES = 2
ALONG_X = 4
ALONG_Y = 4
CHIPS = 32
ALONG_Z = CHIPS // ALONG_X


def own_place():
    place = lax.axis_index("seq")
    return place // (ALONG_Z * CORES), place // CORES % ALONG_Z, place % CORES


def dft_tables(blocks, rows, kept):
    period = 2 * blocks
    length = period * rows
    k1 = np.arange(kept)[:, None]
    used = k1 <= blocks
    angle = 2 * np.pi * ((k1 * np.arange(blocks)[None]) % period) / period
    first = np.concatenate([used * np.cos(angle), used * -np.sin(angle)], 0)
    weight = used * np.where((k1 == 0) | (k1 == blocks), 1.0, 2.0) / length
    last = np.concatenate([(weight * np.cos(angle)).T, -(weight * np.sin(angle)).T], 1)
    turn = 2 * np.pi * (k1 * np.arange(rows)[None]) / length
    twist = np.stack([np.cos(turn), -np.sin(turn)])
    angle = 2 * np.pi * ((np.arange(rows)[:, None] * np.arange(rows)[None]) % rows) / rows
    cos, sin = np.cos(angle), np.sin(angle)
    second = np.block([[cos, -sin], [sin, cos]])
    return first, twist, second, last


def halves(table):
    high = table.astype(BF16)
    low = (table - high.astype(np.float64)).astype(BF16)
    return high, low


def split(value):
    high = value.astype(BF16)
    return high, (value - high.astype(F32)).astype(BF16)


def dot(a, b):
    return jnp.dot(a, b, preferred_element_type=F32)


def dot3(a, b):
    return dot(a[0], b[0]) + (dot(a[0], b[1]) + dot(a[1], b[0]))


def spectrum(data, first_ref, twist_ref, second_ref, chans, rows, kept):
    bins = dot(first_ref[0], data) + dot(first_ref[1], data)
    cos, sin = twist_ref[0], twist_ref[1]
    parts = []
    for c in range(chans):
        re = bins[:kept, c * rows : (c + 1) * rows]
        im = bins[kept:, c * rows : (c + 1) * rows]
        parts.append(jnp.concatenate([re * cos - im * sin, re * sin + im * cos], 1))
    return dot3(split(jnp.concatenate(parts, 0)), (second_ref[0], second_ref[1]))


def by_channel(planes, chips, chans):
    return jnp.concatenate(
        [
            jnp.concatenate(
                [planes[core, pl.ds(c, chips, stride=chans), :] for core in range(CORES)], 0
            )
            for c in range(chans)
        ],
        1,
    ).astype(BF16)


def filter_kernel(sizes, own_ref, came_ref, first_ref, twist_ref, second_ref, out_ref, planes):
    chips, chans, rows, kept = sizes
    odd = own_place()[2] == 1
    own, came = own_ref[...].astype(F32), came_ref[...].astype(F32)
    planes[0] = jnp.where(odd, came, own)
    planes[1] = jnp.where(odd, own, came)
    data = by_channel(planes, chips, chans)
    out_ref[...] = spectrum(data, first_ref, twist_ref, second_ref, chans, rows, kept)


def correlate_kernel(sizes, *refs):
    x_ref, filt_ref, first_ref, twist_ref, second_ref, back_ref, last_ref = refs[1:8]
    kept_ref, *came_refs, out_ref, wide = refs[8:]
    chips, chans, rows, kept = sizes
    came = x_ref[...].astype(F32)
    for core in range(CORES):
        wide[core] = came[:, core * chans : (core + 1) * chans].reshape(chips * chans, rows)
    data = by_channel(wide, chips, chans)
    grads = spectrum(data, first_ref, twist_ref, second_ref, chans, rows, kept)
    g_re, g_im = grads[:, :rows], grads[:, rows:]
    f_re, f_im = filt_ref[:, :rows], filt_ref[:, rows:]
    product = jnp.concatenate([g_re * f_re + g_im * f_im, g_im * f_re - g_re * f_im], 1)
    bins = dot3(split(product), (back_ref[0], back_ref[1]))
    cos, sin = twist_ref[0], twist_ref[1]
    parts = []
    for c in range(chans):
        re = bins[c * kept : (c + 1) * kept, :rows]
        im = bins[c * kept : (c + 1) * kept, rows:]
        parts.append(jnp.concatenate([re * cos + im * sin, im * cos - re * sin], 0))
    inner = dot3((last_ref[0], last_ref[1]), split(jnp.concatenate(parts, 1)))
    for c in range(chans):
        for core in range(CORES):
            wide[core, pl.ds(c, chips, stride=chans), :] = inner[
                core * chips : (core + 1) * chips, c * rows : (c + 1) * rows
            ]
    depth = out_ref.shape[1] - CORES * chans
    came = jnp.concatenate([ref[...] for ref in came_refs], 0)
    total = (kept_ref[...] + came.astype(F32)).astype(BF16)
    out_ref[:, :depth, :] = total.reshape(chips, depth, rows)
    blocks = [wide[core].reshape(chips, chans, rows) for core in range(CORES)]
    out_ref[:, depth:, :] = jnp.concatenate(blocks, 1).astype(BF16)


def pack_kernel(filters_ref, weight_ref, out_ref):
    chips, depth, rows = out_ref.shape
    chan = filters_ref.shape[1]
    feats = weight_ref.shape[0]
    turned = filters_ref[...].astype(F32).T.reshape(CORES, chips, chan // (CORES * chips), rows)
    turned = jnp.swapaxes(turned, 0, 1).reshape(chips, depth - CORES * feats, rows)
    out_ref[:, CORES * feats :, :] = turned.astype(BF16)
    for core in range(CORES):
        for part in range(2):
            start = (core * 2 + part) * rows
            piece = weight_ref[:, start : start + rows]
            for chip in range(chips):
                if chip // ALONG_Z % 2 == part:
                    out_ref[chip, core * feats : (core + 1) * feats, :] = piece


def unpack_kernel(after_ref, came_ref, *out_refs):
    size = out_refs[0].shape[0]
    chips = came_ref.shape[0]
    feats = 2 * size // chips
    odd = own_place()[2] == 1
    for i in range(2):
        place = slice(i * chips // 2, (i + 1) * chips // 2)
        first, second = came_ref[place, :feats, :], came_ref[place, feats : 2 * feats, :]
        out_refs[i][...] = jnp.where(odd, second, first).reshape(size, -1)
        out_refs[2 + i][...] = jnp.where(odd, first, second).reshape(size, -1)


def unpack_filters_kernel(came_ref, own_ref, other_ref):
    chans = own_ref.shape[0] // CHIPS
    odd = own_place()[2] == 1
    came = came_ref[:, -CORES * chans :, :].astype(F32)
    came = came.reshape(CHIPS, CORES, chans, came.shape[2])
    first, second = came[:, 0], came[:, 1]
    own_ref[...] = jnp.where(odd, second, first).reshape(own_ref.shape).astype(BF16)
    other_ref[...] = jnp.where(odd, first, second).reshape(other_ref.shape).astype(BF16)


def left_kernel(mine_ref, theirs_ref, out_ref):
    depth, rows = mine_ref.shape[0] // CORES, mine_ref.shape[1]
    odd = own_place()[2] == 1
    for i, ref in enumerate((mine_ref, theirs_ref)):
        value = ref[...].reshape(CHIPS, CORES, depth // CHIPS, rows)
        first, second = (value[:, core].reshape(depth, rows).astype(F32) for core in range(CORES))
        place = slice(i * rows, (i + 1) * rows)
        out_ref[place, :depth] = jnp.where(odd, second, first).T.astype(BF16)
        out_ref[place, depth:] = jnp.where(odd, first, second).T.astype(BF16)


def halves_kernel(*refs):
    queries_ref, conv_ref, own_ref, other_ref = refs[-4:]
    odd = own_place()[2] == 1
    rows, half = queries_ref.shape[0], own_ref.shape[1]
    for i, ref in enumerate((queries_ref, conv_ref)):
        left, right = ref[:, :half], ref[:, half:]
        own_ref[i * rows : (i + 1) * rows, :] = jnp.where(odd, right, left)
        other_ref[i * rows : (i + 1) * rows, :] = jnp.where(odd, left, right)


def both_cores(own_ref, came_ref):
    rows = own_ref.shape[0] // 2
    own, came = own_ref[...].astype(F32), came_ref[...].astype(F32)
    return (
        jnp.concatenate([own[:rows], came[:rows]], 0),
        jnp.concatenate([own[rows:], came[rows:]], 0),
    )


def gate_kernel(*refs):
    own_ref, came_ref, left_ref, *weight_refs, turned_ref, mine_ref, theirs_ref = refs[-14:]
    x, _, core = own_place()
    odd = core == 1
    rows = mine_ref.shape[0]
    weight = jnp.concatenate(
        [jnp.concatenate([ref[...] for ref in weight_refs[i : i + 4]], 0) for i in (0, 4)], 1
    )
    gate = dot(left_ref[...], weight)
    part = gate.shape[1] // 2
    gate = jnp.where(x % 2 == 1, jnp.concatenate([gate[:, part:], gate[:, :part]], 1), gate)
    queries, conv = both_cores(own_ref, came_ref)
    turned = (gate * queries).astype(BF16).astype(F32).T
    chips, blocks, _ = turned_ref.shape
    own, other = (
        turned[:, i * rows : (i + 1) * rows].reshape(chips, blocks // CORES, rows) for i in range(2)
    )
    turned_ref[...] = jnp.concatenate(
        [jnp.where(odd, other, own), jnp.where(odd, own, other)], 1
    ).astype(BF16)
    query_grad = (gate * conv).astype(BF16)
    mine_ref[...] = query_grad[:rows]
    theirs_ref[...] = query_grad[rows:]


def join_kernel(mine_ref, theirs_ref, out_ref, token_ref):
    token_ref[...] = jnp.zeros_like(token_ref)
    odd = own_place()[2] == 1
    mine, theirs = mine_ref[...], theirs_ref[...]
    half = mine.shape[1]
    out_ref[:, :half] = jnp.where(odd, theirs, mine)
    out_ref[:, half:] = jnp.where(odd, mine, theirs)


def parts_kernel(came_ref, inner_ref, inner_other_ref, weight_ref, weight_other_ref):
    odd = own_place()[2] == 1
    chips, depth, rows = came_ref.shape
    feats = weight_ref.shape[0]
    chans = inner_ref.shape[0] // chips
    inner = came_ref[:, feats:, :].astype(F32).reshape(chips, CORES, chans, rows)
    first, second = (inner[:, core].reshape(chips * chans, rows) for core in range(CORES))
    inner_ref[...] = jnp.where(odd, second, first).astype(BF16)
    inner_other_ref[...] = jnp.where(odd, first, second).astype(BF16)
    sums = came_ref[:, :feats, :].astype(F32)
    sums = sums.reshape(ALONG_X // 2, 2, ALONG_Z // 2, 2, CORES, feats // 2, rows)
    sums = jnp.sum(jnp.sum(sums, 2), 0)
    part = rows // 2
    first, second = (
        jnp.concatenate(
            [
                jnp.concatenate(
                    [
                        sums[x, z, core, :, high * part : (high + 1) * part]
                        for z in range(2)
                        for x in range(2)
                    ],
                    1,
                )
                for high in range(2)
            ],
            0,
        )
        for core in range(CORES)
    )
    weight_ref[...] = jnp.where(odd, second, first)
    weight_other_ref[...] = jnp.where(odd, first, second)


def outputs_kernel(
    scale, own_ref, came_ref, weight_ref, beside_ref, key_ref, value_ref, key_grad_ref, value_grad_ref, weight_grad_ref
):
    odd = own_place()[2] == 1
    half = own_ref.shape[0]
    own, came = own_ref[...].astype(F32).T, came_ref[...].astype(F32).T
    for i, inner in enumerate((jnp.where(odd, came, own), jnp.where(odd, own, came))):
        place = slice(i * half, (i + 1) * half)
        key_grad_ref[:, place] = (inner * value_ref[:, place].astype(F32)).astype(BF16)
        value_grad_ref[:, place] = (inner * key_ref[:, place].astype(F32)).astype(BF16)
    own, came = weight_ref[...] * scale, beside_ref[...] * scale
    weight_grad_ref[:, :half] = jnp.where(odd, came, own)
    weight_grad_ref[:, half:] = jnp.where(odd, own, came)


def arrange_kernel(*refs):
    *block_refs, out_ref = refs[-ALONG_Y - 1 :]
    size = block_refs[0].shape[0]
    for hop, ref in enumerate(block_refs):
        start = pl.multiple_of(lax.rem(lax.axis_index("ch") + hop, ALONG_Y) * size, size)
        out_ref[pl.ds(start, size), :] = ref[...]


def partial_kernel(mine_ref, theirs_ref, own_ref, came_ref, keep_ref, *give_refs):
    queries, conv = both_cores(own_ref, came_ref)
    gated = (queries * conv).astype(BF16)
    part = gated.shape[1] // 2
    upper = own_place()[1] % 2 == 1
    low, high = gated[:, :part], gated[:, part:]
    left = jnp.concatenate([mine_ref[...], theirs_ref[...]], 1)
    keep_ref[...] = dot(left, jnp.where(upper, high, low)).astype(BF16)
    give = dot(left, jnp.where(upper, low, high)).astype(BF16)
    size = give_refs[0].shape[0]
    for i, ref in enumerate(give_refs):
        ref[...] = give[i * size : (i + 1) * size]


def fold_kernel(after_ref, keep_ref, *refs):
    came_refs, (kept_ref, *give_refs) = refs[:1], refs[1:]
    total = keep_ref[...].astype(F32) + jnp.concatenate([ref[...] for ref in came_refs], 0).astype(F32)
    depth, width = total.shape
    total = total.reshape(CORES * CHIPS, 2, depth // (2 * CORES * CHIPS), width)
    first = total[:, 0].reshape(depth // 2, width)
    second = total[:, 1].reshape(depth // 2, width)
    part = width // 2
    low = jnp.concatenate([first[:, :part], second[:, :part]], 1)
    high = jnp.concatenate([first[:, part:], second[:, part:]], 1)
    upper = own_place()[0] % 2 == 1
    kept_ref[...] = jnp.where(upper, high, low)
    give = jnp.where(upper, low, high).astype(BF16)
    size = give_refs[0].shape[0]
    for i, ref in enumerate(give_refs):
        ref[...] = give[i * size : (i + 1) * size]


def in_vmem(count):
    return [pl.BlockSpec(memory_space=pltpu.VMEM)] * count


def call(kernel, out, *operands, scratch=(), after=()):
    return pl.pallas_call(
        kernel,
        out_shape=[jax.ShapeDtypeStruct(shape, dtype) for shape, dtype in out],
        in_specs=[pl.BlockSpec(memory_space=pl.ANY)] * len(after) + in_vmem(len(operands)),
        out_specs=in_vmem(len(out)),
        scratch_shapes=[pltpu.VMEM(shape, F32) for shape in scratch],
        compiler_params=pltpu.CompilerParams(vmem_limit_bytes=10 << 20),
    )(*after, *operands)


def shards(queries, key_proj, value_proj, conv_out, filters, out_grad, out_weight):
    rows, chan = queries.shape
    groups = lax.axis_size("seq")
    feats = out_weight.shape[0]
    chips = groups // CORES
    along_z = chips // ALONG_X
    half = chan // CORES
    chans = chan // groups
    kept = -(-(groups + 1) // 8) * 8
    sizes = (chips, chans, rows, kept)

    def send(value, dx, dz, core):
        pairs = []
        for i in range(groups):
            x, z, c = i // (along_z * CORES), i // CORES % along_z, i % CORES
            x, z, c = (x + dx) % ALONG_X, (z + dz) % along_z, c ^ core
            pairs.append((i, (x * along_z + z) * CORES + c))
        return lax.ppermute(value, "seq", pairs)

    def to_core(value):
        return send(value, 0, 0, 1)

    order = np.arange(groups).reshape(chips, CORES).T.reshape(-1)
    first, twist, second, last = dft_tables(groups, rows, kept)
    first, last = first[:, order], last[order]
    first, last = jnp.stack(halves(first)), jnp.stack(halves(last))
    second, back = jnp.stack(halves(second)), jnp.stack(halves(second.T))
    twist = jnp.asarray(twist, F32)

    (packed,) = call(
        pack_kernel, [((chips, CORES * (feats + chans), rows), BF16)], filters, out_weight
    )
    like_cores = [list(range(core, groups, CORES)) for core in range(CORES)]
    arrived = lax.all_to_all(packed, "seq", 0, 0, axis_index_groups=like_cores)
    halves_own, halves_other = call(
        halves_kernel, [((CORES * rows, half), BF16)] * 2, queries, conv_out
    )

    features = lax.axis_size("ch")
    turned_grad = out_grad.T
    around = [turned_grad] + [
        lax.ppermute(turned_grad, "ch", [(i, (i - hop) % features) for i in range(features)])
        for hop in range(1, features)
    ]
    (wide,) = call(
        arrange_kernel,
        [((groups * feats, rows), BF16)],
        *around,
        after=(halves_own,),
    )
    wide_there = to_core(wide)
    (left,) = call(
        left_kernel, [((CORES * rows, groups * feats), BF16)], wide, wide_there
    )
    halves_came = to_core(halves_other)

    keep, *give = call(
        partial_kernel,
        [((groups * feats, half // 2), BF16)] + [((groups * feats // 1, half // 2), BF16)] * 1,
        wide,
        wide_there,
        halves_own,
        halves_came,
    )
    pieces = call(unpack_kernel, [((chips * feats // 2, rows), BF16)] * 4, arrived, after=(keep,))
    pieces = [*pieces[:2]] + [to_core(piece) for piece in pieces[2:]]
    weights = pieces + [send(piece, 1 - 2 * (i % 2), 0, 0) for i, piece in enumerate(pieces)]
    filters_own, filters_other = call(
        unpack_filters_kernel, [((chips * chans, rows), BF16)] * 2, arrived
    )
    (filt,) = call(
        functools.partial(filter_kernel, sizes),
        [((chans * kept, 2 * rows), F32)],
        filters_own,
        to_core(filters_other),
        first,
        twist,
        second,
        scratch=[(CORES, half, rows)],
    )

    turned, mine, theirs = call(
        gate_kernel,
        [((chips, CORES * chans, rows), BF16)] + [((rows, half), BF16)] * 2,
        halves_own,
        halves_came,
        left,
        *weights,
    )
    keep, *give = call(
        fold_kernel,
        [((groups * feats // 2, half // 2), F32)]
        + [((groups * feats // 4, half // 2), BF16)] * 2,
        keep,
        *[lax.ppermute(value, "seq", [(i, i ^ CORES) for i in range(groups)]) for value in give],
        after=(turned,),
    )
    came = [
        lax.ppermute(value, "seq", [(i, i ^ (along_z * CORES)) for i in range(groups)])
        for value in give
    ]

    received = lax.all_to_all(
        turned,
        "seq",
        0,
        0,
        axis_index_groups=like_cores,
    )
    theirs = to_core(theirs)
    query_grad, joined = call(
        join_kernel, [((rows, chan), BF16), ((8, rows), F32)], mine, theirs
    )
    (inner,) = call(
        functools.partial(correlate_kernel, sizes),
        [((chips, CORES * (feats // 2 + chans), rows), BF16)],
        received,
        filt,
        first,
        twist,
        second,
        back,
        last,
        keep,
        *came,
        scratch=[(CORES, half, rows)],
        after=(joined,),
    )
    inner, inner_other, weight_sum, weight_sum_other = call(
        parts_kernel,
        [((half, rows), BF16)] * 2 + [((feats, half), F32)] * 2,
        lax.all_to_all(inner, "seq", 0, 0, axis_index_groups=like_cores),
    )
    key_grad, value_grad, weight_grad = call(
        functools.partial(outputs_kernel, (rows * groups) ** (-0.5)),
        [((rows, chan), BF16)] * 2 + [((feats, chan), F32)],
        inner,
        to_core(inner_other),
        weight_sum,
        to_core(weight_sum_other),
        key_proj,
        value_proj,
    )
    return (query_grad, key_grad, value_grad, weight_grad)


def solution(mesh):
    placed = (P("seq", "ch"),) * 7
    return jax.shard_map(
        shards,
        mesh=mesh,
        in_specs=placed,
        out_specs=(P("seq", "ch"),) * 4,
        check_vma=False,
    )
```

```python
import functools

import jax
import jax.numpy as jnp
import numpy as np
from jax import lax
from jax.experimental import pallas as pl
from jax.experimental.pallas import tpu as pltpu
from jax.sharding import PartitionSpec as P

BF16 = jnp.bfloat16
F32 = jnp.float32

CORES = 2
ALONG_X = 4
ALONG_Y = 4
CHIPS = 32
ALONG_Z = CHIPS // ALONG_X


def own_place():
    place = lax.axis_index("seq")
    return place // (ALONG_Z * CORES), place // CORES % ALONG_Z, place % CORES


def dft_tables(blocks, rows, kept):
    period = 2 * blocks
    length = period * rows
    k1 = np.arange(kept)[:, None]
    used = k1 <= blocks
    angle = 2 * np.pi * ((k1 * np.arange(blocks)[None]) % period) / period
    first = np.concatenate([used * np.cos(angle), used * -np.sin(angle)], 0)
    weight = used * np.where((k1 == 0) | (k1 == blocks), 1.0, 2.0) / length
    last = np.concatenate([(weight * np.cos(angle)).T, -(weight * np.sin(angle)).T], 1)
    turn = 2 * np.pi * (k1 * np.arange(rows)[None]) / length
    twist = np.stack([np.cos(turn), -np.sin(turn)])
    angle = 2 * np.pi * ((np.arange(rows)[:, None] * np.arange(rows)[None]) % rows) / rows
    cos, sin = np.cos(angle), np.sin(angle)
    second = np.block([[cos, -sin], [sin, cos]])
    return first, twist, second, last


def halves(table):
    high = table.astype(BF16)
    low = (table - high.astype(np.float64)).astype(BF16)
    return high, low


def split(value):
    high = value.astype(BF16)
    return high, (value - high.astype(F32)).astype(BF16)


def dot(a, b):
    return jnp.dot(a, b, preferred_element_type=F32)


def dot3(a, b):
    return dot(a[0], b[0]) + (dot(a[0], b[1]) + dot(a[1], b[0]))


def spectrum(data, first_ref, twist_ref, second_ref, chans, rows, kept):
    bins = dot(first_ref[0], data) + dot(first_ref[1], data)
    cos, sin = twist_ref[0], twist_ref[1]
    parts = []
    for c in range(chans):
        re = bins[:kept, c * rows : (c + 1) * rows]
        im = bins[kept:, c * rows : (c + 1) * rows]
        parts.append(jnp.concatenate([re * cos - im * sin, re * sin + im * cos], 1))
    return dot3(split(jnp.concatenate(parts, 0)), (second_ref[0], second_ref[1]))


def by_channel(planes, chips, chans):
    return jnp.concatenate(
        [
            jnp.concatenate(
                [planes[core, pl.ds(c, chips, stride=chans), :] for core in range(CORES)], 0
            )
            for c in range(chans)
        ],
        1,
    ).astype(BF16)


def filter_kernel(sizes, own_ref, came_ref, first_ref, twist_ref, second_ref, out_ref, planes):
    chips, chans, rows, kept = sizes
    odd = own_place()[2] == 1
    own, came = own_ref[...].astype(F32), came_ref[...].astype(F32)
    planes[0] = jnp.where(odd, came, own)
    planes[1] = jnp.where(odd, own, came)
    data = by_channel(planes, chips, chans)
    out_ref[...] = spectrum(data, first_ref, twist_ref, second_ref, chans, rows, kept)


def correlate_kernel(sizes, *refs):
    x_ref, filt_ref, first_ref, twist_ref, second_ref, back_ref, last_ref = refs[1:8]
    kept_ref, *came_refs, out_ref, wide = refs[8:]
    chips, chans, rows, kept = sizes
    came = x_ref[...].astype(F32)
    for core in range(CORES):
        wide[core] = came[:, core * chans : (core + 1) * chans].reshape(chips * chans, rows)
    data = by_channel(wide, chips, chans)
    grads = spectrum(data, first_ref, twist_ref, second_ref, chans, rows, kept)
    g_re, g_im = grads[:, :rows], grads[:, rows:]
    f_re, f_im = filt_ref[:, :rows], filt_ref[:, rows:]
    product = jnp.concatenate([g_re * f_re + g_im * f_im, g_im * f_re - g_re * f_im], 1)
    bins = dot3(split(product), (back_ref[0], back_ref[1]))
    cos, sin = twist_ref[0], twist_ref[1]
    parts = []
    for c in range(chans):
        re = bins[c * kept : (c + 1) * kept, :rows]
        im = bins[c * kept : (c + 1) * kept, rows:]
        parts.append(jnp.concatenate([re * cos + im * sin, im * cos - re * sin], 0))
    inner = dot3((last_ref[0], last_ref[1]), split(jnp.concatenate(parts, 1)))
    for c in range(chans):
        for core in range(CORES):
            wide[core, pl.ds(c, chips, stride=chans), :] = inner[
                core * chips : (core + 1) * chips, c * rows : (c + 1) * rows
            ]
    depth = out_ref.shape[1] - CORES * chans
    came = jnp.concatenate([ref[...] for ref in came_refs], 0)
    total = (kept_ref[...] + came.astype(F32)).astype(BF16)
    out_ref[:, :depth, :] = total.reshape(chips, depth, rows)
    blocks = [wide[core].reshape(chips, chans, rows) for core in range(CORES)]
    out_ref[:, depth:, :] = jnp.concatenate(blocks, 1).astype(BF16)


def pack_kernel(filters_ref, weight_ref, out_ref):
    chips, depth, rows = out_ref.shape
    chan = filters_ref.shape[1]
    feats = weight_ref.shape[0]
    turned = filters_ref[...].astype(F32).T.reshape(CORES, chips, chan // (CORES * chips), rows)
    turned = jnp.swapaxes(turned, 0, 1).reshape(chips, depth - CORES * feats, rows)
    out_ref[:, CORES * feats :, :] = turned.astype(BF16)
    for core in range(CORES):
        for part in range(2):
            start = (core * 2 + part) * rows
            piece = weight_ref[:, start : start + rows]
            for chip in range(chips):
                if chip // ALONG_Z % 2 == part:
                    out_ref[chip, core * feats : (core + 1) * feats, :] = piece


def unpack_kernel(after_ref, came_ref, *out_refs):
    size = out_refs[0].shape[0]
    chips = came_ref.shape[0]
    feats = 2 * size // chips
    odd = own_place()[2] == 1
    for i in range(2):
        place = slice(i * chips // 2, (i + 1) * chips // 2)
        first, second = came_ref[place, :feats, :], came_ref[place, feats : 2 * feats, :]
        out_refs[i][...] = jnp.where(odd, second, first).reshape(size, -1)
        out_refs[2 + i][...] = jnp.where(odd, first, second).reshape(size, -1)


def unpack_filters_kernel(came_ref, own_ref, other_ref):
    chans = own_ref.shape[0] // CHIPS
    odd = own_place()[2] == 1
    came = came_ref[:, -CORES * chans :, :].astype(F32)
    came = came.reshape(CHIPS, CORES, chans, came.shape[2])
    first, second = came[:, 0], came[:, 1]
    own_ref[...] = jnp.where(odd, second, first).reshape(own_ref.shape).astype(BF16)
    other_ref[...] = jnp.where(odd, first, second).reshape(other_ref.shape).astype(BF16)


def left_kernel(mine_ref, theirs_ref, out_ref):
    depth, rows = mine_ref.shape[0] // CORES, mine_ref.shape[1]
    odd = own_place()[2] == 1
    for i, ref in enumerate((mine_ref, theirs_ref)):
        value = ref[...].reshape(CHIPS, CORES, depth // CHIPS, rows)
        first, second = (value[:, core].reshape(depth, rows).astype(F32) for core in range(CORES))
        place = slice(i * rows, (i + 1) * rows)
        out_ref[place, :depth] = jnp.where(odd, second, first).T.astype(BF16)
        out_ref[place, depth:] = jnp.where(odd, first, second).T.astype(BF16)


def halves_kernel(*refs):
    queries_ref, conv_ref, own_ref, other_ref = refs[-4:]
    odd = own_place()[2] == 1
    rows, half = queries_ref.shape[0], own_ref.shape[1]
    for i, ref in enumerate((queries_ref, conv_ref)):
        left, right = ref[:, :half], ref[:, half:]
        own_ref[i * rows : (i + 1) * rows, :] = jnp.where(odd, right, left)
        other_ref[i * rows : (i + 1) * rows, :] = jnp.where(odd, left, right)


def both_cores(own_ref, came_ref):
    rows = own_ref.shape[0] // 2
    own, came = own_ref[...].astype(F32), came_ref[...].astype(F32)
    return (
        jnp.concatenate([own[:rows], came[:rows]], 0),
        jnp.concatenate([own[rows:], came[rows:]], 0),
    )


def gate_kernel(*refs):
    own_ref, came_ref, left_ref, *weight_refs, turned_ref, mine_ref, theirs_ref = refs[-14:]
    x, _, core = own_place()
    odd = core == 1
    rows = mine_ref.shape[0]
    weight = jnp.concatenate(
        [jnp.concatenate([ref[...] for ref in weight_refs[i : i + 4]], 0) for i in (0, 4)], 1
    )
    gate = dot(left_ref[...], weight)
    part = gate.shape[1] // 2
    gate = jnp.where(x % 2 == 1, jnp.concatenate([gate[:, part:], gate[:, :part]], 1), gate)
    queries, conv = both_cores(own_ref, came_ref)
    turned = (gate * queries).astype(BF16).astype(F32).T
    chips, blocks, _ = turned_ref.shape
    own, other = (
        turned[:, i * rows : (i + 1) * rows].reshape(chips, blocks // CORES, rows) for i in range(2)
    )
    turned_ref[...] = jnp.concatenate(
        [jnp.where(odd, other, own), jnp.where(odd, own, other)], 1
    ).astype(BF16)
    query_grad = (gate * conv).astype(BF16)
    mine_ref[...] = query_grad[:rows]
    theirs_ref[...] = query_grad[rows:]


def parts_kernel(came_ref, inner_ref, inner_other_ref, weight_ref, weight_other_ref):
    odd = own_place()[2] == 1
    chips, depth, rows = came_ref.shape
    feats = weight_ref.shape[0]
    chans = inner_ref.shape[0] // chips
    inner = came_ref[:, feats:, :].astype(F32).reshape(chips, CORES, chans, rows)
    first, second = (inner[:, core].reshape(chips * chans, rows) for core in range(CORES))
    inner_ref[...] = jnp.where(odd, second, first).astype(BF16)
    inner_other_ref[...] = jnp.where(odd, first, second).astype(BF16)
    sums = came_ref[:, :feats, :].astype(F32)
    sums = sums.reshape(ALONG_X // 2, 2, ALONG_Z // 2, 2, CORES, feats // 2, rows)
    sums = jnp.sum(jnp.sum(sums, 2), 0)
    part = rows // 2
    first, second = (
        jnp.concatenate(
            [
                jnp.concatenate(
                    [
                        sums[x, z, core, :, high * part : (high + 1) * part]
                        for z in range(2)
                        for x in range(2)
                    ],
                    1,
                )
                for high in range(2)
            ],
            0,
        )
        for core in range(CORES)
    )
    weight_ref[...] = jnp.where(odd, second, first)
    weight_other_ref[...] = jnp.where(odd, first, second)


def outputs_kernel(scale, *refs):
    odd = own_place()[2] == 1
    own_ref, came_ref, weight_ref, beside_ref, mine_ref, theirs_ref, key_ref, value_ref = refs[:8]
    query_grad_ref, key_grad_ref, value_grad_ref, weight_grad_ref = refs[8:]
    half = own_ref.shape[0]
    own, came = own_ref[...].astype(F32).T, came_ref[...].astype(F32).T
    for i, inner in enumerate((jnp.where(odd, came, own), jnp.where(odd, own, came))):
        place = slice(i * half, (i + 1) * half)
        key_grad_ref[:, place] = (inner * value_ref[:, place].astype(F32)).astype(BF16)
        value_grad_ref[:, place] = (inner * key_ref[:, place].astype(F32)).astype(BF16)
    own, came = weight_ref[...] * scale, beside_ref[...] * scale
    weight_grad_ref[:, :half] = jnp.where(odd, came, own)
    weight_grad_ref[:, half:] = jnp.where(odd, own, came)
    own, came = mine_ref[...], theirs_ref[...]
    query_grad_ref[:, :half] = jnp.where(odd, came, own)
    query_grad_ref[:, half:] = jnp.where(odd, own, came)


def arrange_kernel(*refs):
    *block_refs, out_ref = refs[-ALONG_Y - 1 :]
    size = block_refs[0].shape[0]
    for hop, ref in enumerate(block_refs):
        start = pl.multiple_of(lax.rem(lax.axis_index("ch") + hop, ALONG_Y) * size, size)
        out_ref[pl.ds(start, size), :] = ref[...]


def partial_kernel(mine_ref, theirs_ref, own_ref, came_ref, keep_ref, *give_refs):
    queries, conv = both_cores(own_ref, came_ref)
    gated = (queries * conv).astype(BF16)
    part = gated.shape[1] // 2
    upper = own_place()[1] % 2 == 1
    low, high = gated[:, :part], gated[:, part:]
    left = jnp.concatenate([mine_ref[...], theirs_ref[...]], 1)
    keep_ref[...] = dot(left, jnp.where(upper, high, low)).astype(BF16)
    give = dot(left, jnp.where(upper, low, high)).astype(BF16)
    size = give_refs[0].shape[0]
    for i, ref in enumerate(give_refs):
        ref[...] = give[i * size : (i + 1) * size]


def fold_kernel(after_ref, keep_ref, *refs):
    came_refs, (kept_ref, *give_refs) = refs[:1], refs[1:]
    total = keep_ref[...].astype(F32) + jnp.concatenate([ref[...] for ref in came_refs], 0).astype(F32)
    depth, width = total.shape
    total = total.reshape(CORES * CHIPS, 2, depth // (2 * CORES * CHIPS), width)
    first = total[:, 0].reshape(depth // 2, width)
    second = total[:, 1].reshape(depth // 2, width)
    part = width // 2
    low = jnp.concatenate([first[:, :part], second[:, :part]], 1)
    high = jnp.concatenate([first[:, part:], second[:, part:]], 1)
    upper = own_place()[0] % 2 == 1
    kept_ref[...] = jnp.where(upper, high, low)
    give = jnp.where(upper, low, high).astype(BF16)
    size = give_refs[0].shape[0]
    for i, ref in enumerate(give_refs):
        ref[...] = give[i * size : (i + 1) * size]


def in_vmem(count):
    return [pl.BlockSpec(memory_space=pltpu.VMEM)] * count


def call(kernel, out, *operands, scratch=(), after=()):
    return pl.pallas_call(
        kernel,
        out_shape=[jax.ShapeDtypeStruct(shape, dtype) for shape, dtype in out],
        in_specs=[pl.BlockSpec(memory_space=pl.ANY)] * len(after) + in_vmem(len(operands)),
        out_specs=in_vmem(len(out)),
        scratch_shapes=[pltpu.VMEM(shape, F32) for shape in scratch],
        compiler_params=pltpu.CompilerParams(vmem_limit_bytes=10 << 20),
    )(*after, *operands)


def shards(queries, key_proj, value_proj, conv_out, filters, out_grad, out_weight):
    rows, chan = queries.shape
    groups = lax.axis_size("seq")
    feats = out_weight.shape[0]
    chips = groups // CORES
    along_z = chips // ALONG_X
    half = chan // CORES
    chans = chan // groups
    kept = -(-(groups + 1) // 8) * 8
    sizes = (chips, chans, rows, kept)

    def send(value, dx, dz, core):
        pairs = []
        for i in range(groups):
            x, z, c = i // (along_z * CORES), i // CORES % along_z, i % CORES
            x, z, c = (x + dx) % ALONG_X, (z + dz) % along_z, c ^ core
            pairs.append((i, (x * along_z + z) * CORES + c))
        return lax.ppermute(value, "seq", pairs)

    def to_core(value):
        return send(value, 0, 0, 1)

    order = np.arange(groups).reshape(chips, CORES).T.reshape(-1)
    first, twist, second, last = dft_tables(groups, rows, kept)
    first, last = first[:, order], last[order]
    first, last = jnp.stack(halves(first)), jnp.stack(halves(last))
    second, back = jnp.stack(halves(second)), jnp.stack(halves(second.T))
    twist = jnp.asarray(twist, F32)

    (packed,) = call(
        pack_kernel, [((chips, CORES * (feats + chans), rows), BF16)], filters, out_weight
    )
    like_cores = [list(range(core, groups, CORES)) for core in range(CORES)]
    arrived = lax.all_to_all(packed, "seq", 0, 0, axis_index_groups=like_cores)
    halves_own, halves_other = call(
        halves_kernel, [((CORES * rows, half), BF16)] * 2, queries, conv_out
    )

    features = lax.axis_size("ch")
    turned_grad = out_grad.T
    around = [turned_grad] + [
        lax.ppermute(turned_grad, "ch", [(i, (i - hop) % features) for i in range(features)])
        for hop in range(1, features)
    ]
    (wide,) = call(
        arrange_kernel,
        [((groups * feats, rows), BF16)],
        *around,
        after=(halves_own,),
    )
    wide_there = to_core(wide)
    (left,) = call(
        left_kernel, [((CORES * rows, groups * feats), BF16)], wide, wide_there
    )
    halves_came = to_core(halves_other)

    keep, *give = call(
        partial_kernel,
        [((groups * feats, half // 2), BF16)] + [((groups * feats // 1, half // 2), BF16)] * 1,
        wide,
        wide_there,
        halves_own,
        halves_came,
    )
    pieces = call(unpack_kernel, [((chips * feats // 2, rows), BF16)] * 4, arrived, after=(keep,))
    pieces = [*pieces[:2]] + [to_core(piece) for piece in pieces[2:]]
    weights = pieces + [send(piece, 1 - 2 * (i % 2), 0, 0) for i, piece in enumerate(pieces)]
    filters_own, filters_other = call(
        unpack_filters_kernel, [((chips * chans, rows), BF16)] * 2, arrived
    )
    (filt,) = call(
        functools.partial(filter_kernel, sizes),
        [((chans * kept, 2 * rows), F32)],
        filters_own,
        to_core(filters_other),
        first,
        twist,
        second,
        scratch=[(CORES, half, rows)],
    )

    turned, mine, theirs = call(
        gate_kernel,
        [((chips, CORES * chans, rows), BF16)] + [((rows, half), BF16)] * 2,
        halves_own,
        halves_came,
        left,
        *weights,
    )
    keep, *give = call(
        fold_kernel,
        [((groups * feats // 2, half // 2), F32)]
        + [((groups * feats // 4, half // 2), BF16)] * 2,
        keep,
        *[lax.ppermute(value, "seq", [(i, i ^ CORES) for i in range(groups)]) for value in give],
        after=(turned,),
    )
    came = [send(value, dx, 0, 0) for value, dx in zip(give, (1, -1), strict=True)]

    received = lax.all_to_all(
        turned,
        "seq",
        0,
        0,
        axis_index_groups=like_cores,
    )
    theirs = to_core(theirs)
    (inner,) = call(
        functools.partial(correlate_kernel, sizes),
        [((chips, CORES * (feats // 2 + chans), rows), BF16)],
        received,
        filt,
        first,
        twist,
        second,
        back,
        last,
        keep,
        *came,
        scratch=[(CORES, half, rows)],
        after=(theirs,),
    )
    inner, inner_other, weight_sum, weight_sum_other = call(
        parts_kernel,
        [((half, rows), BF16)] * 2 + [((feats, half), F32)] * 2,
        lax.all_to_all(inner, "seq", 0, 0, axis_index_groups=like_cores),
    )
    return call(
        functools.partial(outputs_kernel, (rows * groups) ** (-0.5)),
        [((rows, chan), BF16)] * 3 + [((feats, chan), F32)],
        inner,
        to_core(inner_other),
        weight_sum,
        to_core(weight_sum_other),
        mine,
        theirs,
        key_proj,
        value_proj,
    )


def solution(mesh):
    placed = (P("seq", "ch"),) * 7
    return jax.shard_map(
        shards,
        mesh=mesh,
        in_specs=placed,
        out_specs=(P("seq", "ch"),) * 4,
        check_vma=False,
    )
```

```python
import functools

import jax
import jax.numpy as jnp
import numpy as np
from jax import lax
from jax.experimental import pallas as pl
from jax.experimental.pallas import tpu as pltpu
from jax.sharding import PartitionSpec as P

BF16 = jnp.bfloat16
F32 = jnp.float32

CORES = 2
ALONG_X = 4
ALONG_Y = 4
CHIPS = 32
ALONG_Z = CHIPS // ALONG_X


def own_place():
    place = lax.axis_index("seq")
    return place // (ALONG_Z * CORES), place // CORES % ALONG_Z, place % CORES


def dft_tables(blocks, rows, kept):
    period = 2 * blocks
    length = period * rows
    k1 = np.arange(kept)[:, None]
    used = k1 <= blocks
    angle = 2 * np.pi * ((k1 * np.arange(blocks)[None]) % period) / period
    first = np.concatenate([used * np.cos(angle), used * -np.sin(angle)], 0)
    weight = used * np.where((k1 == 0) | (k1 == blocks), 1.0, 2.0) / length
    last = np.concatenate([(weight * np.cos(angle)).T, -(weight * np.sin(angle)).T], 1)
    turn = 2 * np.pi * (k1 * np.arange(rows)[None]) / length
    twist = np.stack([np.cos(turn), -np.sin(turn)])
    angle = 2 * np.pi * ((np.arange(rows)[:, None] * np.arange(rows)[None]) % rows) / rows
    cos, sin = np.cos(angle), np.sin(angle)
    second = np.block([[cos, -sin], [sin, cos]])
    return first, twist, second, last


def halves(table):
    high = table.astype(BF16)
    low = (table - high.astype(np.float64)).astype(BF16)
    return high, low


def split(value):
    high = value.astype(BF16)
    return high, (value - high.astype(F32)).astype(BF16)


def dot(a, b):
    return jnp.dot(a, b, preferred_element_type=F32)


def dot3(a, b):
    return dot(a[0], b[0]) + (dot(a[0], b[1]) + dot(a[1], b[0]))


def spectrum(data, first_ref, twist_ref, second_ref, chans, rows, kept):
    bins = dot(first_ref[0], data) + dot(first_ref[1], data)
    cos, sin = twist_ref[0], twist_ref[1]
    parts = []
    for c in range(chans):
        re = bins[:kept, c * rows : (c + 1) * rows]
        im = bins[kept:, c * rows : (c + 1) * rows]
        parts.append(jnp.concatenate([re * cos - im * sin, re * sin + im * cos], 1))
    return dot3(split(jnp.concatenate(parts, 0)), (second_ref[0], second_ref[1]))


def by_channel(planes, chips, chans):
    return jnp.concatenate(
        [
            jnp.concatenate(
                [planes[core, pl.ds(c, chips, stride=chans), :] for core in range(CORES)], 0
            )
            for c in range(chans)
        ],
        1,
    ).astype(BF16)


def filter_kernel(sizes, own_ref, came_ref, first_ref, twist_ref, second_ref, out_ref, planes):
    chips, chans, rows, kept = sizes
    odd = own_place()[2] == 1
    own, came = own_ref[...].astype(F32), came_ref[...].astype(F32)
    planes[0] = jnp.where(odd, came, own)
    planes[1] = jnp.where(odd, own, came)
    data = by_channel(planes, chips, chans)
    out_ref[...] = spectrum(data, first_ref, twist_ref, second_ref, chans, rows, kept)


def correlate_kernel(sizes, *refs):
    x_ref, filt_ref, first_ref, twist_ref, second_ref, back_ref, last_ref = refs[1:8]
    kept_ref, *came_refs, out_ref, wide = refs[8:]
    chips, chans, rows, kept = sizes
    came = x_ref[...].astype(F32)
    for core in range(CORES):
        wide[core] = came[:, core * chans : (core + 1) * chans].reshape(chips * chans, rows)
    data = by_channel(wide, chips, chans)
    grads = spectrum(data, first_ref, twist_ref, second_ref, chans, rows, kept)
    g_re, g_im = grads[:, :rows], grads[:, rows:]
    f_re, f_im = filt_ref[:, :rows], filt_ref[:, rows:]
    product = jnp.concatenate([g_re * f_re + g_im * f_im, g_im * f_re - g_re * f_im], 1)
    bins = dot3(split(product), (back_ref[0], back_ref[1]))
    cos, sin = twist_ref[0], twist_ref[1]
    parts = []
    for c in range(chans):
        re = bins[c * kept : (c + 1) * kept, :rows]
        im = bins[c * kept : (c + 1) * kept, rows:]
        parts.append(jnp.concatenate([re * cos + im * sin, im * cos - re * sin], 0))
    inner = dot3((last_ref[0], last_ref[1]), split(jnp.concatenate(parts, 1)))
    for c in range(chans):
        for core in range(CORES):
            wide[core, pl.ds(c, chips, stride=chans), :] = inner[
                core * chips : (core + 1) * chips, c * rows : (c + 1) * rows
            ]
    depth = out_ref.shape[1] - CORES * chans
    came = jnp.concatenate([ref[...] for ref in came_refs], 0)
    total = (kept_ref[...] + came.astype(F32)).astype(BF16)
    out_ref[:, :depth, :] = total.reshape(chips, depth, rows)
    blocks = [wide[core].reshape(chips, chans, rows) for core in range(CORES)]
    out_ref[:, depth:, :] = jnp.concatenate(blocks, 1).astype(BF16)


def pack_kernel(filters_ref, weight_ref, out_ref):
    chips, depth, rows = out_ref.shape
    chan = filters_ref.shape[1]
    feats = weight_ref.shape[1]
    turned = filters_ref[...].astype(F32).T.reshape(CORES, chips, chan // (CORES * chips), rows)
    turned = jnp.swapaxes(turned, 0, 1).reshape(chips, depth - CORES * feats, rows)
    out_ref[:, CORES * feats :, :] = turned.astype(BF16)
    for core in range(CORES):
        for part in range(2):
            piece = weight_ref[core * 2 + part]
            for chip in range(chips):
                if chip // ALONG_Z % 2 == part:
                    out_ref[chip, core * feats : (core + 1) * feats, :] = piece


def unpack_kernel(after_ref, came_ref, *out_refs):
    size = out_refs[0].shape[0]
    chips = came_ref.shape[0]
    feats = 2 * size // chips
    odd = own_place()[2] == 1
    for i in range(2):
        place = slice(i * chips // 2, (i + 1) * chips // 2)
        first, second = came_ref[place, :feats, :], came_ref[place, feats : 2 * feats, :]
        out_refs[i][...] = jnp.where(odd, second, first).reshape(size, -1)
        out_refs[2 + i][...] = jnp.where(odd, first, second).reshape(size, -1)


def unpack_filters_kernel(came_ref, own_ref, other_ref):
    chans = own_ref.shape[0] // CHIPS
    odd = own_place()[2] == 1
    came = came_ref[:, -CORES * chans :, :].astype(F32)
    came = came.reshape(CHIPS, CORES, chans, came.shape[2])
    first, second = came[:, 0], came[:, 1]
    own_ref[...] = jnp.where(odd, second, first).reshape(own_ref.shape).astype(BF16)
    other_ref[...] = jnp.where(odd, first, second).reshape(other_ref.shape).astype(BF16)


def left_kernel(mine_ref, theirs_ref, out_ref):
    depth, rows = mine_ref.shape[0] // CORES, mine_ref.shape[1]
    odd = own_place()[2] == 1
    for i, ref in enumerate((mine_ref, theirs_ref)):
        value = ref[...].reshape(CHIPS, CORES, depth // CHIPS, rows)
        first, second = (value[:, core].reshape(depth, rows).astype(F32) for core in range(CORES))
        place = slice(i * rows, (i + 1) * rows)
        out_ref[place, :depth] = jnp.where(odd, second, first).T.astype(BF16)
        out_ref[place, depth:] = jnp.where(odd, first, second).T.astype(BF16)


def halves_kernel(*refs):
    queries_ref, conv_ref, own_ref, other_ref = refs[-4:]
    odd = own_place()[2] == 1
    rows, half = queries_ref.shape[0], own_ref.shape[1]
    for i, ref in enumerate((queries_ref, conv_ref)):
        left, right = ref[:, :half], ref[:, half:]
        own_ref[i * rows : (i + 1) * rows, :] = jnp.where(odd, right, left)
        other_ref[i * rows : (i + 1) * rows, :] = jnp.where(odd, left, right)


def both_cores(own_ref, came_ref):
    rows = own_ref.shape[0] // 2
    own, came = own_ref[...].astype(F32), came_ref[...].astype(F32)
    return (
        jnp.concatenate([own[:rows], came[:rows]], 0),
        jnp.concatenate([own[rows:], came[rows:]], 0),
    )


def gate_kernel(*refs):
    own_ref, came_ref, left_ref, *weight_refs, turned_ref, mine_ref, theirs_ref = refs[-14:]
    x, _, core = own_place()
    odd = core == 1
    rows = mine_ref.shape[0]
    weight = jnp.concatenate(
        [jnp.concatenate([ref[...] for ref in weight_refs[i : i + 4]], 0) for i in (0, 4)], 1
    )
    gate = dot(left_ref[...], weight)
    part = gate.shape[1] // 2
    gate = jnp.where(x % 2 == 1, jnp.concatenate([gate[:, part:], gate[:, :part]], 1), gate)
    queries, conv = both_cores(own_ref, came_ref)
    turned = (gate * queries).astype(BF16).astype(F32).T
    chips, blocks, _ = turned_ref.shape
    own, other = (
        turned[:, i * rows : (i + 1) * rows].reshape(chips, blocks // CORES, rows) for i in range(2)
    )
    turned_ref[...] = jnp.concatenate(
        [jnp.where(odd, other, own), jnp.where(odd, own, other)], 1
    ).astype(BF16)
    query_grad = (gate * conv).astype(BF16)
    mine_ref[...] = query_grad[:rows]
    theirs_ref[...] = query_grad[rows:]


def parts_kernel(came_ref, inner_ref, inner_other_ref, weight_ref, weight_other_ref):
    odd = own_place()[2] == 1
    chips, depth, rows = came_ref.shape
    feats = weight_ref.shape[0]
    chans = inner_ref.shape[0] // chips
    inner = came_ref[:, feats:, :].astype(F32).reshape(chips, CORES, chans, rows)
    first, second = (inner[:, core].reshape(chips * chans, rows) for core in range(CORES))
    inner_ref[...] = jnp.where(odd, second, first).astype(BF16)
    inner_other_ref[...] = jnp.where(odd, first, second).astype(BF16)
    sums = came_ref[:, :feats, :].astype(F32)
    sums = sums.reshape(ALONG_X // 2, 2, ALONG_Z // 2, 2, CORES, feats // 2, rows)
    sums = jnp.sum(jnp.sum(sums, 2), 0)
    part = rows // 2
    first, second = (
        jnp.concatenate(
            [
                jnp.concatenate(
                    [
                        sums[x, z, core, :, high * part : (high + 1) * part]
                        for z in range(2)
                        for x in range(2)
                    ],
                    1,
                )
                for high in range(2)
            ],
            0,
        )
        for core in range(CORES)
    )
    weight_ref[...] = jnp.where(odd, second, first)
    weight_other_ref[...] = jnp.where(odd, first, second)


def outputs_kernel(scale, *refs):
    odd = own_place()[2] == 1
    own_ref, came_ref, weight_ref, beside_ref, mine_ref, theirs_ref, key_ref, value_ref = refs[:8]
    query_grad_ref, key_grad_ref, value_grad_ref, weight_grad_ref = refs[8:]
    half = own_ref.shape[0]
    own, came = own_ref[...].astype(F32).T, came_ref[...].astype(F32).T
    for i, inner in enumerate((jnp.where(odd, came, own), jnp.where(odd, own, came))):
        place = slice(i * half, (i + 1) * half)
        key_grad_ref[:, place] = (inner * value_ref[:, place].astype(F32)).astype(BF16)
        value_grad_ref[:, place] = (inner * key_ref[:, place].astype(F32)).astype(BF16)
    own, came = weight_ref[...] * scale, beside_ref[...] * scale
    weight_grad_ref[:, :half] = jnp.where(odd, came, own)
    weight_grad_ref[:, half:] = jnp.where(odd, own, came)
    own, came = mine_ref[...], theirs_ref[...]
    query_grad_ref[:, :half] = jnp.where(odd, came, own)
    query_grad_ref[:, half:] = jnp.where(odd, own, came)


def arrange_kernel(*refs):
    *block_refs, out_ref = refs[-ALONG_Y - 1 :]
    size = block_refs[0].shape[0]
    for hop, ref in enumerate(block_refs):
        start = pl.multiple_of(lax.rem(lax.axis_index("ch") + hop, ALONG_Y) * size, size)
        out_ref[pl.ds(start, size), :] = ref[...]


def partial_kernel(mine_ref, theirs_ref, own_ref, came_ref, keep_ref, *give_refs):
    queries, conv = both_cores(own_ref, came_ref)
    gated = (queries * conv).astype(BF16)
    part = gated.shape[1] // 2
    upper = own_place()[1] % 2 == 1
    low, high = gated[:, :part], gated[:, part:]
    left = jnp.concatenate([mine_ref[...], theirs_ref[...]], 1)
    keep_ref[...] = dot(left, jnp.where(upper, high, low)).astype(BF16)
    give = dot(left, jnp.where(upper, low, high)).astype(BF16)
    size = give_refs[0].shape[0]
    for i, ref in enumerate(give_refs):
        ref[...] = give[i * size : (i + 1) * size]


def fold_kernel(after_ref, keep_ref, *refs):
    came_refs, (kept_ref, *give_refs) = refs[:1], refs[1:]
    total = keep_ref[...].astype(F32) + jnp.concatenate([ref[...] for ref in came_refs], 0).astype(F32)
    depth, width = total.shape
    total = total.reshape(CORES * CHIPS, 2, depth // (2 * CORES * CHIPS), width)
    first = total[:, 0].reshape(depth // 2, width)
    second = total[:, 1].reshape(depth // 2, width)
    part = width // 2
    low = jnp.concatenate([first[:, :part], second[:, :part]], 1)
    high = jnp.concatenate([first[:, part:], second[:, part:]], 1)
    upper = own_place()[0] % 2 == 1
    kept_ref[...] = jnp.where(upper, high, low)
    give = jnp.where(upper, low, high).astype(BF16)
    size = give_refs[0].shape[0]
    for i, ref in enumerate(give_refs):
        ref[...] = give[i * size : (i + 1) * size]


def in_vmem(count):
    return [pl.BlockSpec(memory_space=pltpu.VMEM)] * count


def call(kernel, out, *operands, scratch=(), after=()):
    return pl.pallas_call(
        kernel,
        out_shape=[jax.ShapeDtypeStruct(shape, dtype) for shape, dtype in out],
        in_specs=[pl.BlockSpec(memory_space=pl.ANY)] * len(after) + in_vmem(len(operands)),
        out_specs=in_vmem(len(out)),
        scratch_shapes=[pltpu.VMEM(shape, F32) for shape in scratch],
        compiler_params=pltpu.CompilerParams(vmem_limit_bytes=10 << 20),
    )(*after, *operands)


def shards(queries, key_proj, value_proj, conv_out, filters, out_grad, out_weight):
    rows, chan = queries.shape
    groups = lax.axis_size("seq")
    feats = out_weight.shape[0]
    chips = groups // CORES
    along_z = chips // ALONG_X
    half = chan // CORES
    chans = chan // groups
    kept = -(-(groups + 1) // 8) * 8
    sizes = (chips, chans, rows, kept)

    def send(value, dx, dz, core):
        pairs = []
        for i in range(groups):
            x, z, c = i // (along_z * CORES), i // CORES % along_z, i % CORES
            x, z, c = (x + dx) % ALONG_X, (z + dz) % along_z, c ^ core
            pairs.append((i, (x * along_z + z) * CORES + c))
        return lax.ppermute(value, "seq", pairs)

    def to_core(value):
        return send(value, 0, 0, 1)

    order = np.arange(groups).reshape(chips, CORES).T.reshape(-1)
    first, twist, second, last = dft_tables(groups, rows, kept)
    first, last = first[:, order], last[order]
    first, last = jnp.stack(halves(first)), jnp.stack(halves(last))
    second, back = jnp.stack(halves(second)), jnp.stack(halves(second.T))
    twist = jnp.asarray(twist, F32)

    (packed,) = call(
        pack_kernel,
        [((chips, CORES * (feats + chans), rows), BF16)],
        filters,
        out_weight.reshape(feats, CORES * 2, rows).swapaxes(0, 1),
    )
    like_cores = [list(range(core, groups, CORES)) for core in range(CORES)]
    arrived = lax.all_to_all(packed, "seq", 0, 0, axis_index_groups=like_cores)
    halves_own, halves_other = call(
        halves_kernel, [((CORES * rows, half), BF16)] * 2, queries, conv_out
    )

    features = lax.axis_size("ch")
    turned_grad = out_grad.T
    around = [turned_grad] + [
        lax.ppermute(turned_grad, "ch", [(i, (i - hop) % features) for i in range(features)])
        for hop in range(1, features)
    ]
    (wide,) = call(
        arrange_kernel,
        [((groups * feats, rows), BF16)],
        *around,
        after=(halves_own,),
    )
    wide_there = to_core(wide)
    (left,) = call(
        left_kernel, [((CORES * rows, groups * feats), BF16)], wide, wide_there
    )
    halves_came = to_core(halves_other)

    keep, *give = call(
        partial_kernel,
        [((groups * feats, half // 2), BF16)] + [((groups * feats // 1, half // 2), BF16)] * 1,
        wide,
        wide_there,
        halves_own,
        halves_came,
    )
    pieces = call(unpack_kernel, [((chips * feats // 2, rows), BF16)] * 4, arrived, after=(keep,))
    pieces = [*pieces[:2]] + [to_core(piece) for piece in pieces[2:]]
    weights = pieces + [send(piece, 1 - 2 * (i % 2), 0, 0) for i, piece in enumerate(pieces)]
    filters_own, filters_other = call(
        unpack_filters_kernel, [((chips * chans, rows), BF16)] * 2, arrived
    )
    (filt,) = call(
        functools.partial(filter_kernel, sizes),
        [((chans * kept, 2 * rows), F32)],
        filters_own,
        to_core(filters_other),
        first,
        twist,
        second,
        scratch=[(CORES, half, rows)],
    )

    turned, mine, theirs = call(
        gate_kernel,
        [((chips, CORES * chans, rows), BF16)] + [((rows, half), BF16)] * 2,
        halves_own,
        halves_came,
        left,
        *weights,
    )
    keep, *give = call(
        fold_kernel,
        [((groups * feats // 2, half // 2), F32)]
        + [((groups * feats // 4, half // 2), BF16)] * 2,
        keep,
        *[lax.ppermute(value, "seq", [(i, i ^ CORES) for i in range(groups)]) for value in give],
        after=(turned,),
    )
    came = [send(value, dx, 0, 0) for value, dx in zip(give, (1, -1), strict=True)]

    received = lax.all_to_all(
        turned,
        "seq",
        0,
        0,
        axis_index_groups=like_cores,
    )
    theirs = to_core(theirs)
    (inner,) = call(
        functools.partial(correlate_kernel, sizes),
        [((chips, CORES * (feats // 2 + chans), rows), BF16)],
        received,
        filt,
        first,
        twist,
        second,
        back,
        last,
        keep,
        *came,
        scratch=[(CORES, half, rows)],
        after=(theirs,),
    )
    inner, inner_other, weight_sum, weight_sum_other = call(
        parts_kernel,
        [((half, rows), BF16)] * 2 + [((feats, half), F32)] * 2,
        lax.all_to_all(inner, "seq", 0, 0, axis_index_groups=like_cores),
    )
    return call(
        functools.partial(outputs_kernel, (rows * groups) ** (-0.5)),
        [((rows, chan), BF16)] * 3 + [((feats, chan), F32)],
        inner,
        to_core(inner_other),
        weight_sum,
        to_core(weight_sum_other),
        mine,
        theirs,
        key_proj,
        value_proj,
    )


def solution(mesh):
    placed = (P("seq", "ch"),) * 7
    return jax.shard_map(
        shards,
        mesh=mesh,
        in_specs=placed,
        out_specs=(P("seq", "ch"),) * 4,
        check_vma=False,
    )
```

```python
import functools

import jax
import jax.numpy as jnp
import numpy as np
from jax import lax
from jax.experimental import pallas as pl
from jax.experimental.pallas import tpu as pltpu
from jax.sharding import PartitionSpec as P

BF16 = jnp.bfloat16
F32 = jnp.float32

CORES = 2
ALONG_X = 4
ALONG_Y = 4
CHIPS = 32
ALONG_Z = CHIPS // ALONG_X


def own_place():
    place = lax.axis_index("seq")
    return place // (ALONG_Z * CORES), place // CORES % ALONG_Z, place % CORES


def dft_tables(blocks, rows, kept):
    period = 2 * blocks
    length = period * rows
    k1 = np.arange(kept)[:, None]
    used = k1 <= blocks
    angle = 2 * np.pi * ((k1 * np.arange(blocks)[None]) % period) / period
    first = np.concatenate([used * np.cos(angle), used * -np.sin(angle)], 0)
    weight = used * np.where((k1 == 0) | (k1 == blocks), 1.0, 2.0) / length
    last = np.concatenate([(weight * np.cos(angle)).T, -(weight * np.sin(angle)).T], 1)
    turn = 2 * np.pi * (k1 * np.arange(rows)[None]) / length
    twist = np.stack([np.cos(turn), -np.sin(turn)])
    angle = 2 * np.pi * ((np.arange(rows)[:, None] * np.arange(rows)[None]) % rows) / rows
    cos, sin = np.cos(angle), np.sin(angle)
    second = np.block([[cos, -sin], [sin, cos]])
    return first, twist, second, last


def halves(table):
    high = table.astype(BF16)
    low = (table - high.astype(np.float64)).astype(BF16)
    return high, low


def split(value):
    high = value.astype(BF16)
    return high, (value - high.astype(F32)).astype(BF16)


def dot(a, b):
    return jnp.dot(a, b, preferred_element_type=F32)


def dot3(a, b):
    return dot(a[0], b[0]) + (dot(a[0], b[1]) + dot(a[1], b[0]))


def spectrum(data, first_ref, twist_ref, second_ref, chans, rows, kept):
    bins = dot(first_ref[...], jnp.concatenate([data, data], 0))
    cos, sin = twist_ref[0], twist_ref[1]
    parts = []
    for c in range(chans):
        re = bins[:kept, c * rows : (c + 1) * rows]
        im = bins[kept:, c * rows : (c + 1) * rows]
        parts.append(jnp.concatenate([re * cos - im * sin, re * sin + im * cos], 1))
    return dot3(split(jnp.concatenate(parts, 0)), (second_ref[0], second_ref[1]))


def by_channel(planes, chips, chans):
    return jnp.concatenate(
        [
            jnp.concatenate(
                [planes[core, pl.ds(c, chips, stride=chans), :] for core in range(CORES)], 0
            )
            for c in range(chans)
        ],
        1,
    ).astype(BF16)


def filter_kernel(sizes, own_ref, came_ref, first_ref, twist_ref, second_ref, out_ref, planes):
    chips, chans, rows, kept = sizes
    odd = own_place()[2] == 1
    own, came = own_ref[...].astype(F32), came_ref[...].astype(F32)
    planes[0] = jnp.where(odd, came, own)
    planes[1] = jnp.where(odd, own, came)
    data = by_channel(planes, chips, chans)
    out_ref[...] = spectrum(data, first_ref, twist_ref, second_ref, chans, rows, kept)


def correlate_kernel(sizes, *refs):
    x_ref, filt_ref, first_ref, twist_ref, second_ref, back_ref, last_ref = refs[1:8]
    kept_ref, *came_refs, out_ref, wide = refs[8:]
    chips, chans, rows, kept = sizes
    came = x_ref[...].astype(F32)
    for core in range(CORES):
        wide[core] = came[:, core * chans : (core + 1) * chans].reshape(chips * chans, rows)
    data = by_channel(wide, chips, chans)
    grads = spectrum(data, first_ref, twist_ref, second_ref, chans, rows, kept)
    g_re, g_im = grads[:, :rows], grads[:, rows:]
    f_re, f_im = filt_ref[:, :rows], filt_ref[:, rows:]
    product = jnp.concatenate([g_re * f_re + g_im * f_im, g_im * f_re - g_re * f_im], 1)
    bins = dot3(split(product), (back_ref[0], back_ref[1]))
    cos, sin = twist_ref[0], twist_ref[1]
    parts = []
    for c in range(chans):
        re = bins[c * kept : (c + 1) * kept, :rows]
        im = bins[c * kept : (c + 1) * kept, rows:]
        parts.append(jnp.concatenate([re * cos + im * sin, im * cos - re * sin], 0))
    high, low = split(jnp.concatenate(parts, 1))
    inner = dot(last_ref[...], jnp.concatenate([high, high, low], 0))
    for c in range(chans):
        for core in range(CORES):
            wide[core, pl.ds(c, chips, stride=chans), :] = inner[
                core * chips : (core + 1) * chips, c * rows : (c + 1) * rows
            ]
    depth = out_ref.shape[1] - CORES * chans
    came = jnp.concatenate([ref[...] for ref in came_refs], 0)
    total = (kept_ref[...] + came.astype(F32)).astype(BF16)
    out_ref[:, :depth, :] = total.reshape(chips, depth, rows)
    blocks = [wide[core].reshape(chips, chans, rows) for core in range(CORES)]
    out_ref[:, depth:, :] = jnp.concatenate(blocks, 1).astype(BF16)


def pack_kernel(filters_ref, weight_ref, out_ref):
    chips, depth, rows = out_ref.shape
    chan = filters_ref.shape[1]
    feats = weight_ref.shape[1]
    turned = filters_ref[...].astype(F32).T.reshape(CORES, chips, chan // (CORES * chips), rows)
    turned = jnp.swapaxes(turned, 0, 1).reshape(chips, depth - CORES * feats, rows)
    out_ref[:, CORES * feats :, :] = turned.astype(BF16)
    for core in range(CORES):
        for part in range(2):
            piece = weight_ref[core * 2 + part]
            for chip in range(chips):
                if chip // ALONG_Z % 2 == part:
                    out_ref[chip, core * feats : (core + 1) * feats, :] = piece


def unpack_kernel(after_ref, came_ref, *out_refs):
    size = out_refs[0].shape[0]
    chips = came_ref.shape[0]
    feats = 2 * size // chips
    odd = own_place()[2] == 1
    for i in range(2):
        place = slice(i * chips // 2, (i + 1) * chips // 2)
        first, second = came_ref[place, :feats, :], came_ref[place, feats : 2 * feats, :]
        out_refs[i][...] = jnp.where(odd, second, first).reshape(size, -1)
        out_refs[2 + i][...] = jnp.where(odd, first, second).reshape(size, -1)


def unpack_filters_kernel(came_ref, own_ref, other_ref):
    chans = own_ref.shape[0] // CHIPS
    odd = own_place()[2] == 1
    came = came_ref[:, -CORES * chans :, :].astype(F32)
    came = came.reshape(CHIPS, CORES, chans, came.shape[2])
    first, second = came[:, 0], came[:, 1]
    own_ref[...] = jnp.where(odd, second, first).reshape(own_ref.shape).astype(BF16)
    other_ref[...] = jnp.where(odd, first, second).reshape(other_ref.shape).astype(BF16)


def left_kernel(mine_ref, theirs_ref, out_ref):
    depth, rows = mine_ref.shape[0] // CORES, mine_ref.shape[1]
    odd = own_place()[2] == 1
    for i, ref in enumerate((mine_ref, theirs_ref)):
        value = ref[...].reshape(CHIPS, CORES, depth // CHIPS, rows)
        first, second = (value[:, core].reshape(depth, rows).astype(F32) for core in range(CORES))
        place = slice(i * rows, (i + 1) * rows)
        out_ref[place, :depth] = jnp.where(odd, second, first).T.astype(BF16)
        out_ref[place, depth:] = jnp.where(odd, first, second).T.astype(BF16)


def halves_kernel(*refs):
    queries_ref, conv_ref, own_ref, other_ref = refs[-4:]
    odd = own_place()[2] == 1
    rows, half = queries_ref.shape[0], own_ref.shape[1]
    for i, ref in enumerate((queries_ref, conv_ref)):
        left, right = ref[:, :half], ref[:, half:]
        own_ref[i * rows : (i + 1) * rows, :] = jnp.where(odd, right, left)
        other_ref[i * rows : (i + 1) * rows, :] = jnp.where(odd, left, right)


def both_cores(own_ref, came_ref):
    rows = own_ref.shape[0] // 2
    own, came = own_ref[...].astype(F32), came_ref[...].astype(F32)
    return (
        jnp.concatenate([own[:rows], came[:rows]], 0),
        jnp.concatenate([own[rows:], came[rows:]], 0),
    )


def gate_kernel(*refs):
    own_ref, came_ref, left_ref, *weight_refs, turned_ref, mine_ref, theirs_ref = refs[-14:]
    x, _, core = own_place()
    odd = core == 1
    rows = mine_ref.shape[0]
    weight = jnp.concatenate(
        [jnp.concatenate([ref[...] for ref in weight_refs[i : i + 4]], 0) for i in (0, 4)], 1
    )
    gate = dot(left_ref[...], weight)
    part = gate.shape[1] // 2
    gate = jnp.where(x % 2 == 1, jnp.concatenate([gate[:, part:], gate[:, :part]], 1), gate)
    queries, conv = both_cores(own_ref, came_ref)
    turned = (gate * queries).astype(BF16).astype(F32).T
    chips, blocks, _ = turned_ref.shape
    own, other = (
        turned[:, i * rows : (i + 1) * rows].reshape(chips, blocks // CORES, rows) for i in range(2)
    )
    turned_ref[...] = jnp.concatenate(
        [jnp.where(odd, other, own), jnp.where(odd, own, other)], 1
    ).astype(BF16)
    query_grad = (gate * conv).astype(BF16)
    mine_ref[...] = query_grad[:rows]
    theirs_ref[...] = query_grad[rows:]


def parts_kernel(came_ref, inner_ref, inner_other_ref, weight_ref, weight_other_ref):
    odd = own_place()[2] == 1
    chips, depth, rows = came_ref.shape
    feats = weight_ref.shape[0]
    chans = inner_ref.shape[0] // chips
    inner = came_ref[:, feats:, :].astype(F32).reshape(chips, CORES, chans, rows)
    first, second = (inner[:, core].reshape(chips * chans, rows) for core in range(CORES))
    inner_ref[...] = jnp.where(odd, second, first).astype(BF16)
    inner_other_ref[...] = jnp.where(odd, first, second).astype(BF16)
    sums = came_ref[:, :feats, :].astype(F32)
    sums = sums.reshape(ALONG_X // 2, 2, ALONG_Z // 2, 2, CORES, feats // 2, rows)
    sums = jnp.sum(jnp.sum(sums, 2), 0)
    part = rows // 2
    first, second = (
        jnp.concatenate(
            [
                jnp.concatenate(
                    [
                        sums[x, z, core, :, high * part : (high + 1) * part]
                        for z in range(2)
                        for x in range(2)
                    ],
                    1,
                )
                for high in range(2)
            ],
            0,
        )
        for core in range(CORES)
    )
    weight_ref[...] = jnp.where(odd, second, first)
    weight_other_ref[...] = jnp.where(odd, first, second)


def outputs_kernel(scale, *refs):
    odd = own_place()[2] == 1
    own_ref, came_ref, weight_ref, beside_ref, mine_ref, theirs_ref, key_ref, value_ref = refs[:8]
    query_grad_ref, key_grad_ref, value_grad_ref, weight_grad_ref = refs[8:]
    half = own_ref.shape[0]
    own, came = own_ref[...].astype(F32).T, came_ref[...].astype(F32).T
    for i, inner in enumerate((jnp.where(odd, came, own), jnp.where(odd, own, came))):
        place = slice(i * half, (i + 1) * half)
        key_grad_ref[:, place] = (inner * value_ref[:, place].astype(F32)).astype(BF16)
        value_grad_ref[:, place] = (inner * key_ref[:, place].astype(F32)).astype(BF16)
    own, came = weight_ref[...] * scale, beside_ref[...] * scale
    weight_grad_ref[:, :half] = jnp.where(odd, came, own)
    weight_grad_ref[:, half:] = jnp.where(odd, own, came)
    own, came = mine_ref[...], theirs_ref[...]
    query_grad_ref[:, :half] = jnp.where(odd, came, own)
    query_grad_ref[:, half:] = jnp.where(odd, own, came)


def arrange_kernel(*refs):
    *block_refs, out_ref = refs[-ALONG_Y - 1 :]
    size = block_refs[0].shape[0]
    for hop, ref in enumerate(block_refs):
        start = pl.multiple_of(lax.rem(lax.axis_index("ch") + hop, ALONG_Y) * size, size)
        out_ref[pl.ds(start, size), :] = ref[...]


def partial_kernel(mine_ref, theirs_ref, own_ref, came_ref, keep_ref, *give_refs):
    queries, conv = both_cores(own_ref, came_ref)
    gated = (queries * conv).astype(BF16)
    part = gated.shape[1] // 2
    upper = own_place()[1] % 2 == 1
    low, high = gated[:, :part], gated[:, part:]
    left = jnp.concatenate([mine_ref[...], theirs_ref[...]], 1)
    keep_ref[...] = dot(left, jnp.where(upper, high, low)).astype(BF16)
    give = dot(left, jnp.where(upper, low, high)).astype(BF16)
    size = give_refs[0].shape[0]
    for i, ref in enumerate(give_refs):
        ref[...] = give[i * size : (i + 1) * size]


def fold_kernel(after_ref, keep_ref, *refs):
    came_refs, (kept_ref, *give_refs) = refs[:1], refs[1:]
    total = keep_ref[...].astype(F32) + jnp.concatenate([ref[...] for ref in came_refs], 0).astype(F32)
    depth, width = total.shape
    total = total.reshape(CORES * CHIPS, 2, depth // (2 * CORES * CHIPS), width)
    first = total[:, 0].reshape(depth // 2, width)
    second = total[:, 1].reshape(depth // 2, width)
    part = width // 2
    low = jnp.concatenate([first[:, :part], second[:, :part]], 1)
    high = jnp.concatenate([first[:, part:], second[:, part:]], 1)
    upper = own_place()[0] % 2 == 1
    kept_ref[...] = jnp.where(upper, high, low)
    give = jnp.where(upper, low, high).astype(BF16)
    size = give_refs[0].shape[0]
    for i, ref in enumerate(give_refs):
        ref[...] = give[i * size : (i + 1) * size]


def in_vmem(count):
    return [pl.BlockSpec(memory_space=pltpu.VMEM)] * count


def call(kernel, out, *operands, scratch=(), after=()):
    return pl.pallas_call(
        kernel,
        out_shape=[jax.ShapeDtypeStruct(shape, dtype) for shape, dtype in out],
        in_specs=[pl.BlockSpec(memory_space=pl.ANY)] * len(after) + in_vmem(len(operands)),
        out_specs=in_vmem(len(out)),
        scratch_shapes=[pltpu.VMEM(shape, F32) for shape in scratch],
        compiler_params=pltpu.CompilerParams(vmem_limit_bytes=10 << 20),
    )(*after, *operands)


def shards(queries, key_proj, value_proj, conv_out, filters, out_grad, out_weight):
    rows, chan = queries.shape
    groups = lax.axis_size("seq")
    feats = out_weight.shape[0]
    chips = groups // CORES
    along_z = chips // ALONG_X
    half = chan // CORES
    chans = chan // groups
    kept = -(-(groups + 1) // 8) * 8
    sizes = (chips, chans, rows, kept)

    def send(value, dx, dz, core):
        pairs = []
        for i in range(groups):
            x, z, c = i // (along_z * CORES), i // CORES % along_z, i % CORES
            x, z, c = (x + dx) % ALONG_X, (z + dz) % along_z, c ^ core
            pairs.append((i, (x * along_z + z) * CORES + c))
        return lax.ppermute(value, "seq", pairs)

    def to_core(value):
        return send(value, 0, 0, 1)

    order = np.arange(groups).reshape(chips, CORES).T.reshape(-1)
    first, twist, second, last = dft_tables(groups, rows, kept)
    first, last = first[:, order], last[order]
    first = jnp.concatenate(halves(first), 1)
    high, low = halves(last)
    last = jnp.concatenate([high, low, high], 1)
    second, back = jnp.stack(halves(second)), jnp.stack(halves(second.T))
    twist = jnp.asarray(twist, F32)

    (packed,) = call(
        pack_kernel,
        [((chips, CORES * (feats + chans), rows), BF16)],
        filters,
        out_weight.reshape(feats, CORES * 2, rows).swapaxes(0, 1),
    )
    like_cores = [list(range(core, groups, CORES)) for core in range(CORES)]
    arrived = lax.all_to_all(packed, "seq", 0, 0, axis_index_groups=like_cores)
    halves_own, halves_other = call(
        halves_kernel, [((CORES * rows, half), BF16)] * 2, queries, conv_out
    )

    features = lax.axis_size("ch")
    turned_grad = out_grad.T
    around = [turned_grad] + [
        lax.ppermute(turned_grad, "ch", [(i, (i - hop) % features) for i in range(features)])
        for hop in range(1, features)
    ]
    (wide,) = call(
        arrange_kernel,
        [((groups * feats, rows), BF16)],
        *around,
        after=(halves_own,),
    )
    wide_there = to_core(wide)
    (left,) = call(
        left_kernel, [((CORES * rows, groups * feats), BF16)], wide, wide_there
    )
    halves_came = to_core(halves_other)

    keep, *give = call(
        partial_kernel,
        [((groups * feats, half // 2), BF16)] + [((groups * feats // 1, half // 2), BF16)] * 1,
        wide,
        wide_there,
        halves_own,
        halves_came,
    )
    pieces = call(unpack_kernel, [((chips * feats // 2, rows), BF16)] * 4, arrived, after=(keep,))
    pieces = [*pieces[:2]] + [to_core(piece) for piece in pieces[2:]]
    weights = pieces + [send(piece, 1 - 2 * (i % 2), 0, 0) for i, piece in enumerate(pieces)]
    filters_own, filters_other = call(
        unpack_filters_kernel, [((chips * chans, rows), BF16)] * 2, arrived
    )
    (filt,) = call(
        functools.partial(filter_kernel, sizes),
        [((chans * kept, 2 * rows), F32)],
        filters_own,
        to_core(filters_other),
        first,
        twist,
        second,
        scratch=[(CORES, half, rows)],
    )

    turned, mine, theirs = call(
        gate_kernel,
        [((chips, CORES * chans, rows), BF16)] + [((rows, half), BF16)] * 2,
        halves_own,
        halves_came,
        left,
        *weights,
    )
    keep, *give = call(
        fold_kernel,
        [((groups * feats // 2, half // 2), F32)]
        + [((groups * feats // 4, half // 2), BF16)] * 2,
        keep,
        *[lax.ppermute(value, "seq", [(i, i ^ CORES) for i in range(groups)]) for value in give],
        after=(turned,),
    )
    came = [send(value, dx, 0, 0) for value, dx in zip(give, (1, -1), strict=True)]

    received = lax.all_to_all(
        turned,
        "seq",
        0,
        0,
        axis_index_groups=like_cores,
    )
    theirs = to_core(theirs)
    (inner,) = call(
        functools.partial(correlate_kernel, sizes),
        [((chips, CORES * (feats // 2 + chans), rows), BF16)],
        received,
        filt,
        first,
        twist,
        second,
        back,
        last,
        keep,
        *came,
        scratch=[(CORES, half, rows)],
        after=(theirs,),
    )
    inner, inner_other, weight_sum, weight_sum_other = call(
        parts_kernel,
        [((half, rows), BF16)] * 2 + [((feats, half), F32)] * 2,
        lax.all_to_all(inner, "seq", 0, 0, axis_index_groups=like_cores),
    )
    return call(
        functools.partial(outputs_kernel, (rows * groups) ** (-0.5)),
        [((rows, chan), BF16)] * 3 + [((feats, chan), F32)],
        inner,
        to_core(inner_other),
        weight_sum,
        to_core(weight_sum_other),
        mine,
        theirs,
        key_proj,
        value_proj,
    )


def solution(mesh):
    placed = (P("seq", "ch"),) * 7
    return jax.shard_map(
        shards,
        mesh=mesh,
        in_specs=placed,
        out_specs=(P("seq", "ch"),) * 4,
        check_vma=False,
    )
```

```python
import functools

import jax
import jax.numpy as jnp
import numpy as np
from jax import lax
from jax.experimental import pallas as pl
from jax.experimental.pallas import tpu as pltpu
from jax.sharding import PartitionSpec as P

BF16 = jnp.bfloat16
F32 = jnp.float32

CORES = 2
ALONG_X = 4
ALONG_Y = 4
CHIPS = 32
ALONG_Z = CHIPS // ALONG_X


def own_place():
    place = lax.axis_index("seq")
    return place // (ALONG_Z * CORES), place // CORES % ALONG_Z, place % CORES


def dft_tables(blocks, rows, kept):
    period = 2 * blocks
    length = period * rows
    k1 = np.arange(kept)[:, None]
    used = k1 <= blocks
    angle = 2 * np.pi * ((k1 * np.arange(blocks)[None]) % period) / period
    first = np.concatenate([used * np.cos(angle), used * -np.sin(angle)], 0)
    weight = used * np.where((k1 == 0) | (k1 == blocks), 1.0, 2.0) / length
    last = np.concatenate([(weight * np.cos(angle)).T, -(weight * np.sin(angle)).T], 1)
    turn = 2 * np.pi * (k1 * np.arange(rows)[None]) / length
    twist = np.stack([np.cos(turn), -np.sin(turn)])
    angle = 2 * np.pi * ((np.arange(rows)[:, None] * np.arange(rows)[None]) % rows) / rows
    cos, sin = np.cos(angle), np.sin(angle)
    second = np.block([[cos, -sin], [sin, cos]])
    return first, twist, second, last


def halves(table):
    high = table.astype(BF16)
    low = (table - high.astype(np.float64)).astype(BF16)
    return high, low


def split(value):
    high = value.astype(BF16)
    return high, (value - high.astype(F32)).astype(BF16)


def dot(a, b):
    return jnp.dot(a, b, preferred_element_type=F32)


def dot3(a, b):
    return dot(a[0], b[0]) + (dot(a[0], b[1]) + dot(a[1], b[0]))


def spectrum(data, first_ref, twist_ref, second_ref, chans, rows, kept):
    bins = dot(first_ref[...], jnp.concatenate([data, data], 0))
    cos, sin = twist_ref[0], twist_ref[1]
    parts = []
    for c in range(chans):
        re = bins[:kept, c * rows : (c + 1) * rows]
        im = bins[kept:, c * rows : (c + 1) * rows]
        parts.append(jnp.concatenate([re * cos - im * sin, re * sin + im * cos], 1))
    return dot3(split(jnp.concatenate(parts, 0)), (second_ref[0], second_ref[1]))


def by_channel(planes, chips, chans):
    return jnp.concatenate(
        [
            jnp.concatenate(
                [planes[core, pl.ds(c, chips, stride=chans), :] for core in range(CORES)], 0
            )
            for c in range(chans)
        ],
        1,
    ).astype(BF16)


def filter_kernel(sizes, own_ref, came_ref, first_ref, twist_ref, second_ref, out_ref, planes):
    chips, chans, rows, kept = sizes
    odd = own_place()[2] == 1
    own, came = own_ref[...].astype(F32), came_ref[...].astype(F32)
    planes[0] = jnp.where(odd, came, own)
    planes[1] = jnp.where(odd, own, came)
    data = by_channel(planes, chips, chans)
    out_ref[...] = spectrum(data, first_ref, twist_ref, second_ref, chans, rows, kept)


def correlate_kernel(sizes, *refs):
    x_ref, filt_ref, first_ref, twist_ref, second_ref, back_ref, last_ref = refs[1:8]
    kept_ref, *came_refs, out_ref, wide = refs[8:]
    chips, chans, rows, kept = sizes
    came = x_ref[...].astype(F32)
    for core in range(CORES):
        wide[core] = came[:, core * chans : (core + 1) * chans].reshape(chips * chans, rows)
    data = by_channel(wide, chips, chans)
    grads = spectrum(data, first_ref, twist_ref, second_ref, chans, rows, kept)
    g_re, g_im = grads[:, :rows], grads[:, rows:]
    f_re, f_im = filt_ref[:, :rows], filt_ref[:, rows:]
    product = jnp.concatenate([g_re * f_re + g_im * f_im, g_im * f_re - g_re * f_im], 1)
    bins = dot3(split(product), (back_ref[0], back_ref[1]))
    cos, sin = twist_ref[0], twist_ref[1]
    parts = []
    for c in range(chans):
        re = bins[c * kept : (c + 1) * kept, :rows]
        im = bins[c * kept : (c + 1) * kept, rows:]
        parts.append(jnp.concatenate([re * cos + im * sin, im * cos - re * sin], 0))
    high, low = split(jnp.concatenate(parts, 1))
    inner = dot(last_ref[...], jnp.concatenate([high, high, low], 0))
    for c in range(chans):
        for core in range(CORES):
            wide[core, pl.ds(c, chips, stride=chans), :] = inner[
                core * chips : (core + 1) * chips, c * rows : (c + 1) * rows
            ]
    depth = out_ref.shape[1] - CORES * chans
    came = jnp.concatenate([ref[...] for ref in came_refs], 0)
    total = (kept_ref[...] + came.astype(F32)).astype(BF16)
    out_ref[:, :depth, :] = total.reshape(chips, depth, rows)
    blocks = [wide[core].reshape(chips, chans, rows) for core in range(CORES)]
    out_ref[:, depth:, :] = jnp.concatenate(blocks, 1).astype(BF16)


def pack_kernel(filters_ref, weight_ref, out_ref):
    chips, depth, rows = out_ref.shape
    chan = filters_ref.shape[1]
    feats = weight_ref.shape[1]
    turned = filters_ref[...].astype(F32).T.reshape(CORES, chips, chan // (CORES * chips), rows)
    turned = jnp.swapaxes(turned, 0, 1).reshape(chips, depth - CORES * feats, rows)
    out_ref[:, CORES * feats :, :] = turned.astype(BF16)
    for core in range(CORES):
        for part in range(2):
            piece = weight_ref[core * 2 + part]
            for chip in range(chips):
                if chip // ALONG_Z % 2 == part:
                    out_ref[chip, core * feats : (core + 1) * feats, :] = piece


def unpack_kernel(after_ref, came_ref, *out_refs):
    size = out_refs[0].shape[0]
    chips = came_ref.shape[0]
    feats = 2 * size // chips
    odd = own_place()[2] == 1
    for i in range(2):
        place = slice(i * chips // 2, (i + 1) * chips // 2)
        first, second = came_ref[place, :feats, :], came_ref[place, feats : 2 * feats, :]
        out_refs[i][...] = jnp.where(odd, second, first).reshape(size, -1)
        out_refs[2 + i][...] = jnp.where(odd, first, second).reshape(size, -1)


def unpack_filters_kernel(came_ref, own_ref, other_ref):
    chans = own_ref.shape[0] // CHIPS
    odd = own_place()[2] == 1
    came = came_ref[:, -CORES * chans :, :].astype(F32)
    came = came.reshape(CHIPS, CORES, chans, came.shape[2])
    first, second = came[:, 0], came[:, 1]
    own_ref[...] = jnp.where(odd, second, first).reshape(own_ref.shape).astype(BF16)
    other_ref[...] = jnp.where(odd, first, second).reshape(other_ref.shape).astype(BF16)


def left_kernel(mine_ref, theirs_ref, out_ref):
    depth, rows = mine_ref.shape[0] // CORES, mine_ref.shape[1]
    odd = own_place()[2] == 1
    for i, ref in enumerate((mine_ref, theirs_ref)):
        value = ref[...].reshape(CHIPS, CORES, depth // CHIPS, rows)
        first, second = (value[:, core].reshape(depth, rows).astype(F32) for core in range(CORES))
        place = slice(i * rows, (i + 1) * rows)
        out_ref[place, :depth] = jnp.where(odd, second, first).T.astype(BF16)
        out_ref[place, depth:] = jnp.where(odd, first, second).T.astype(BF16)


def halves_kernel(*refs):
    queries_ref, conv_ref, own_ref, other_ref = refs[-4:]
    odd = own_place()[2] == 1
    rows, half = queries_ref.shape[0], own_ref.shape[1]
    for i, ref in enumerate((queries_ref, conv_ref)):
        left, right = ref[:, :half], ref[:, half:]
        own_ref[i * rows : (i + 1) * rows, :] = jnp.where(odd, right, left)
        other_ref[i * rows : (i + 1) * rows, :] = jnp.where(odd, left, right)


def both_cores(own_ref, came_ref):
    rows = own_ref.shape[0] // 2
    own, came = own_ref[...].astype(F32), came_ref[...].astype(F32)
    return (
        jnp.concatenate([own[:rows], came[:rows]], 0),
        jnp.concatenate([own[rows:], came[rows:]], 0),
    )


def gate_kernel(*refs):
    own_ref, came_ref, left_ref, *weight_refs, turned_ref, mine_ref, theirs_ref = refs[-14:]
    x, _, core = own_place()
    odd = core == 1
    rows = mine_ref.shape[0]
    weight = jnp.concatenate(
        [jnp.concatenate([ref[...] for ref in weight_refs[i : i + 4]], 0) for i in (0, 4)], 1
    )
    gate = dot(left_ref[...], weight)
    part = gate.shape[1] // 2
    gate = jnp.where(x % 2 == 1, jnp.concatenate([gate[:, part:], gate[:, :part]], 1), gate)
    queries, conv = both_cores(own_ref, came_ref)
    turned = (gate * queries).astype(BF16).astype(F32).T
    chips, blocks, _ = turned_ref.shape
    own, other = (
        turned[:, i * rows : (i + 1) * rows].reshape(chips, blocks // CORES, rows) for i in range(2)
    )
    turned_ref[...] = jnp.concatenate(
        [jnp.where(odd, other, own), jnp.where(odd, own, other)], 1
    ).astype(BF16)
    query_grad = (gate * conv).astype(BF16)
    mine_ref[...] = query_grad[:rows]
    theirs_ref[...] = query_grad[rows:]


def parts_kernel(came_ref, inner_ref, inner_other_ref, weight_ref, weight_other_ref):
    odd = own_place()[2] == 1
    chips, depth, rows = came_ref.shape
    feats = weight_ref.shape[0]
    chans = inner_ref.shape[0] // chips
    inner = came_ref[:, feats:, :].astype(F32).reshape(chips, CORES, chans, rows)
    first, second = (inner[:, core].reshape(chips * chans, rows) for core in range(CORES))
    inner_ref[...] = jnp.where(odd, second, first).astype(BF16)
    inner_other_ref[...] = jnp.where(odd, first, second).astype(BF16)
    sums = came_ref[:, :feats, :].astype(F32)
    sums = sums.reshape(ALONG_X // 2, 2, ALONG_Z // 2, 2, CORES, feats // 2, rows)
    sums = jnp.sum(jnp.sum(sums, 2), 0)
    part = rows // 2
    first, second = (
        jnp.concatenate(
            [
                jnp.concatenate(
                    [
                        sums[x, z, core, :, high * part : (high + 1) * part]
                        for z in range(2)
                        for x in range(2)
                    ],
                    1,
                )
                for high in range(2)
            ],
            0,
        )
        for core in range(CORES)
    )
    weight_ref[...] = jnp.where(odd, second, first)
    weight_other_ref[...] = jnp.where(odd, first, second)


def own_outputs_kernel(own_ref, mine_ref, theirs_ref, key_ref, value_ref, query_grad_ref, key_own_ref, value_own_ref):
    odd = own_place()[2] == 1
    half = own_ref.shape[0]
    inner = own_ref[...].astype(F32).T
    for ref, out_ref in ((value_ref, key_own_ref), (key_ref, value_own_ref)):
        factor = jnp.where(odd, ref[:, half:], ref[:, :half])
        out_ref[...] = (inner * factor.astype(F32)).astype(BF16)
    own, came = mine_ref[...], theirs_ref[...]
    query_grad_ref[:, :half] = jnp.where(odd, came, own)
    query_grad_ref[:, half:] = jnp.where(odd, own, came)


def outputs_kernel(scale, *refs):
    odd = own_place()[2] == 1
    key_own_ref, value_own_ref, came_ref, weight_ref, beside_ref, key_ref, value_ref = refs[:7]
    key_grad_ref, value_grad_ref, weight_grad_ref = refs[7:]
    half = came_ref.shape[0]
    inner = came_ref[...].astype(F32).T
    for ref, own_ref, out_ref in (
        (value_ref, key_own_ref, key_grad_ref),
        (key_ref, value_own_ref, value_grad_ref),
    ):
        factor = jnp.where(odd, ref[:, :half], ref[:, half:])
        came, own = (inner * factor.astype(F32)).astype(BF16), own_ref[...]
        out_ref[:, :half] = jnp.where(odd, came, own)
        out_ref[:, half:] = jnp.where(odd, own, came)
    own, came = weight_ref[...] * scale, beside_ref[...] * scale
    weight_grad_ref[:, :half] = jnp.where(odd, came, own)
    weight_grad_ref[:, half:] = jnp.where(odd, own, came)


def arrange_kernel(*refs):
    *block_refs, out_ref = refs[-ALONG_Y - 1 :]
    size = block_refs[0].shape[0]
    for hop, ref in enumerate(block_refs):
        start = pl.multiple_of(lax.rem(lax.axis_index("ch") + hop, ALONG_Y) * size, size)
        out_ref[pl.ds(start, size), :] = ref[...]


def partial_kernel(mine_ref, theirs_ref, own_ref, came_ref, keep_ref, *give_refs):
    queries, conv = both_cores(own_ref, came_ref)
    gated = (queries * conv).astype(BF16)
    part = gated.shape[1] // 2
    upper = own_place()[1] % 2 == 1
    low, high = gated[:, :part], gated[:, part:]
    left = jnp.concatenate([mine_ref[...], theirs_ref[...]], 1)
    keep_ref[...] = dot(left, jnp.where(upper, high, low)).astype(BF16)
    give = dot(left, jnp.where(upper, low, high)).astype(BF16)
    size = give_refs[0].shape[0]
    for i, ref in enumerate(give_refs):
        ref[...] = give[i * size : (i + 1) * size]


def fold_kernel(after_ref, keep_ref, *refs):
    came_refs, (kept_ref, *give_refs) = refs[:1], refs[1:]
    total = keep_ref[...].astype(F32) + jnp.concatenate([ref[...] for ref in came_refs], 0).astype(F32)
    depth, width = total.shape
    total = total.reshape(CORES * CHIPS, 2, depth // (2 * CORES * CHIPS), width)
    first = total[:, 0].reshape(depth // 2, width)
    second = total[:, 1].reshape(depth // 2, width)
    part = width // 2
    low = jnp.concatenate([first[:, :part], second[:, :part]], 1)
    high = jnp.concatenate([first[:, part:], second[:, part:]], 1)
    upper = own_place()[0] % 2 == 1
    kept_ref[...] = jnp.where(upper, high, low)
    give = jnp.where(upper, low, high).astype(BF16)
    size = give_refs[0].shape[0]
    for i, ref in enumerate(give_refs):
        ref[...] = give[i * size : (i + 1) * size]


def in_vmem(count):
    return [pl.BlockSpec(memory_space=pltpu.VMEM)] * count


def call(kernel, out, *operands, scratch=(), after=()):
    return pl.pallas_call(
        kernel,
        out_shape=[jax.ShapeDtypeStruct(shape, dtype) for shape, dtype in out],
        in_specs=[pl.BlockSpec(memory_space=pl.ANY)] * len(after) + in_vmem(len(operands)),
        out_specs=in_vmem(len(out)),
        scratch_shapes=[pltpu.VMEM(shape, F32) for shape in scratch],
        compiler_params=pltpu.CompilerParams(vmem_limit_bytes=10 << 20),
    )(*after, *operands)


def shards(queries, key_proj, value_proj, conv_out, filters, out_grad, out_weight):
    rows, chan = queries.shape
    groups = lax.axis_size("seq")
    feats = out_weight.shape[0]
    chips = groups // CORES
    along_z = chips // ALONG_X
    half = chan // CORES
    chans = chan // groups
    kept = -(-(groups + 1) // 8) * 8
    sizes = (chips, chans, rows, kept)

    def send(value, dx, dz, core):
        pairs = []
        for i in range(groups):
            x, z, c = i // (along_z * CORES), i // CORES % along_z, i % CORES
            x, z, c = (x + dx) % ALONG_X, (z + dz) % along_z, c ^ core
            pairs.append((i, (x * along_z + z) * CORES + c))
        return lax.ppermute(value, "seq", pairs)

    def to_core(value):
        return send(value, 0, 0, 1)

    order = np.arange(groups).reshape(chips, CORES).T.reshape(-1)
    first, twist, second, last = dft_tables(groups, rows, kept)
    first, last = first[:, order], last[order]
    first = jnp.concatenate(halves(first), 1)
    high, low = halves(last)
    last = jnp.concatenate([high, low, high], 1)
    second, back = jnp.stack(halves(second)), jnp.stack(halves(second.T))
    twist = jnp.asarray(twist, F32)

    (packed,) = call(
        pack_kernel,
        [((chips, CORES * (feats + chans), rows), BF16)],
        filters,
        out_weight.reshape(feats, CORES * 2, rows).swapaxes(0, 1),
    )
    like_cores = [list(range(core, groups, CORES)) for core in range(CORES)]
    arrived = lax.all_to_all(packed, "seq", 0, 0, axis_index_groups=like_cores)
    halves_own, halves_other = call(
        halves_kernel, [((CORES * rows, half), BF16)] * 2, queries, conv_out
    )

    features = lax.axis_size("ch")
    turned_grad = out_grad.T
    around = [turned_grad] + [
        lax.ppermute(turned_grad, "ch", [(i, (i - hop) % features) for i in range(features)])
        for hop in range(1, features)
    ]
    (wide,) = call(
        arrange_kernel,
        [((groups * feats, rows), BF16)],
        *around,
        after=(halves_own,),
    )
    wide_there = to_core(wide)
    (left,) = call(
        left_kernel, [((CORES * rows, groups * feats), BF16)], wide, wide_there
    )
    halves_came = to_core(halves_other)

    keep, *give = call(
        partial_kernel,
        [((groups * feats, half // 2), BF16)] + [((groups * feats // 1, half // 2), BF16)] * 1,
        wide,
        wide_there,
        halves_own,
        halves_came,
    )
    pieces = call(unpack_kernel, [((chips * feats // 2, rows), BF16)] * 4, arrived, after=(keep,))
    pieces = [*pieces[:2]] + [to_core(piece) for piece in pieces[2:]]
    weights = pieces + [send(piece, 1 - 2 * (i % 2), 0, 0) for i, piece in enumerate(pieces)]
    filters_own, filters_other = call(
        unpack_filters_kernel, [((chips * chans, rows), BF16)] * 2, arrived
    )
    (filt,) = call(
        functools.partial(filter_kernel, sizes),
        [((chans * kept, 2 * rows), F32)],
        filters_own,
        to_core(filters_other),
        first,
        twist,
        second,
        scratch=[(CORES, half, rows)],
    )

    turned, mine, theirs = call(
        gate_kernel,
        [((chips, CORES * chans, rows), BF16)] + [((rows, half), BF16)] * 2,
        halves_own,
        halves_came,
        left,
        *weights,
    )
    keep, *give = call(
        fold_kernel,
        [((groups * feats // 2, half // 2), F32)]
        + [((groups * feats // 4, half // 2), BF16)] * 2,
        keep,
        *[lax.ppermute(value, "seq", [(i, i ^ CORES) for i in range(groups)]) for value in give],
        after=(turned,),
    )
    came = [send(value, dx, 0, 0) for value, dx in zip(give, (1, -1), strict=True)]

    received = lax.all_to_all(
        turned,
        "seq",
        0,
        0,
        axis_index_groups=like_cores,
    )
    theirs = to_core(theirs)
    (inner,) = call(
        functools.partial(correlate_kernel, sizes),
        [((chips, CORES * (feats // 2 + chans), rows), BF16)],
        received,
        filt,
        first,
        twist,
        second,
        back,
        last,
        keep,
        *came,
        scratch=[(CORES, half, rows)],
        after=(theirs,),
    )
    inner, inner_other, weight_sum, weight_sum_other = call(
        parts_kernel,
        [((half, rows), BF16)] * 2 + [((feats, half), F32)] * 2,
        lax.all_to_all(inner, "seq", 0, 0, axis_index_groups=like_cores),
    )
    query_grad, key_own, value_own = call(
        own_outputs_kernel,
        [((rows, chan), BF16)] + [((rows, half), BF16)] * 2,
        inner,
        mine,
        theirs,
        key_proj,
        value_proj,
    )
    key_grad, value_grad, weight_grad = call(
        functools.partial(outputs_kernel, (rows * groups) ** (-0.5)),
        [((rows, chan), BF16)] * 2 + [((feats, chan), F32)],
        key_own,
        value_own,
        to_core(inner_other),
        weight_sum,
        to_core(weight_sum_other),
        key_proj,
        value_proj,
    )
    return query_grad, key_grad, value_grad, weight_grad


def solution(mesh):
    placed = (P("seq", "ch"),) * 7
    return jax.shard_map(
        shards,
        mesh=mesh,
        in_specs=placed,
        out_specs=(P("seq", "ch"),) * 4,
        check_vma=False,
    )
```
